32 devices in a mesh: tm: 4 (over y, x), chan: 8 (over z, core).
Axes of the slice: x: 2, y: 2, z: 4, core: 2. Of those that a mesh axis runs over, the one named last changes fastest.
Arguments:
- latent_input: bfloat16 [2048, 320], P('chan', 'tm'), may hold values from -6 to 6
- upsample_kernel: bfloat16 [16, 1024, 2048], P(None, 'chan', 'tm'), may hold values from -0.09375 to 0.09375
- dilated_kernel: bfloat16 [2, 7, 1024, 1024], P(None, None, 'chan'), may hold values from -0.0625 to 0.0625
- pointwise_kernel: bfloat16 [2, 1024, 1024], P(None, 'chan'), may hold values from -0.1875 to 0.1875
- dilated_prune_mask: int32 [2, 7, 1024, 128], P(None, None, 'chan'), may hold values 0 or 1
- pointwise_prune_mask: int32 [2, 1024, 128], P(None, 'chan'), may hold values 0 or 1
- snake_freq_upsample: float32 [2048], P('chan'), may hold values from 0.5 to 3
- snake_freq_dilated: float32 [2, 1024], P(None, 'chan'), may hold values from 0.5 to 3
- snake_freq_pointwise: float32 [2, 1024], P(None, 'chan'), may hold values from 0.5 to 3
- segment_lengths: int32 [3], replicated, may hold values from 1 to 240, as said below
- cotangent: bfloat16 [1024, 2560], P('chan', 'tm'), may hold values from -6 to 6
Outputs:
- decoded: bfloat16 [1024, 2560], P('chan', 'tm')
- dil_saliency: float32 [2, 7, 1024, 1024], P(None, None, 'chan')
- point_saliency: float32 [2, 1024, 1024], P(None, 'chan')
The draws below stay inside these ranges and needn't reach their ends.
Inputs may be any that keep to these rules, and one draw needn't show every extreme that they name: `segment_lengths`: 3 lengths in latent frames that sum to 320, in an order drawn with them; the longest is exactly 240.
All inputs are finite; a program needn't handle non-finite values. No bound on the sum of `dilated_prune_mask` or of `pointwise_prune_mask` on one device may be relied on, other than what follows from the above.
Results may differ from the reference program's by a relative error of at most 0.035.
Values may be sent and summed in bfloat16 or wider, within the bound.
A program may use at most 128 MiB of HBM per device.

```python
import math
import jax
import jax.numpy as jnp
from jax import lax

D_IN = 2048
OUTPUT_CHANNELS = 1024
STRIDE = 8
KT = 16
DILATED_TAPS = 7
RESIDUAL_COUNT = 2
PRUNE_CHANNELS = 8
FR_DEV = 80
FRAMES = 320
ROWS = 2560
N_CHAN = 8


def draw_segment_lengths(key, part):
    longest = FRAMES // 2 + FR_DEV
    length_key = jax.random.fold_in(key, 11)
    order_key = jax.random.fold_in(key, 23)
    first_length = jax.random.randint(length_key, (), 1, FRAMES // 2 - FR_DEV, dtype=jnp.int32)
    middle_length = jnp.zeros((), jnp.int32) + longest
    last_length = FRAMES - longest - first_length
    lengths = jnp.stack([first_length, middle_length, last_length]).astype(jnp.int32)
    order = jax.random.permutation(order_key, 3)
    return lengths[order].astype(jnp.int32)


def place_ends(drawn, stream_key, low, largest):
    dims = drawn.shape
    place = [jax.random.randint(jax.random.fold_in(stream_key, axis), (), 0, dims[axis]) for axis in range(len(dims))]
    drawn = drawn.at[tuple(place)].set(low)
    longest = dims.index(max(dims))
    place[longest] = (place[longest] + 1) % dims[longest]
    return drawn.at[tuple(place)].set(largest)


def levels(key, dims, pieces, low, largest):
    level = 1.0
    for position, shards_of in pieces:
        steps = jax.random.uniform(jax.random.fold_in(jax.random.fold_in(key, 6), position), (shards_of,), jnp.float32, low / len(pieces), largest / len(pieces))
        level = level * jnp.repeat(jnp.exp(steps), dims[position] // shards_of).reshape((-1,) + (1,) * (len(dims) - 1 - position))
    return level


def noise(stream_key, shape, spread, reach, pieces=(), kind=jnp.bfloat16):
    level = levels(stream_key, shape, pieces, -0.22, 0.18) if pieces else 1.0
    entries = jax.random.normal(stream_key, shape, jnp.float32) * spread * level
    return jnp.minimum(jnp.maximum(entries, -reach), reach).astype(kind)


def setup_inputs(seed: int = 0) -> dict:
    key_of = jax.random.split(jax.random.key(seed), 12)
    latent_input = noise(key_of[0], (D_IN, FRAMES), 1.0, 6.0, ((0, 8), (1, 4)))
    upsample_kernel = noise(key_of[1], (KT, OUTPUT_CHANNELS, D_IN), (2 * D_IN) ** -0.5, 0.09375, ((1, 8), (2, 4)))
    dilated_kernel = noise(key_of[2], (RESIDUAL_COUNT, DILATED_TAPS, OUTPUT_CHANNELS, OUTPUT_CHANNELS), (DILATED_TAPS * OUTPUT_CHANNELS) ** -0.5, 0.0625, ((2, 8),))
    pointwise_kernel = noise(key_of[3], (RESIDUAL_COUNT, OUTPUT_CHANNELS, OUTPUT_CHANNELS), OUTPUT_CHANNELS ** -0.5, 0.1875, ((1, 8),))
    dilated_prune_mask = place_ends((jax.random.randint(key_of[4], (RESIDUAL_COUNT, DILATED_TAPS, OUTPUT_CHANNELS, OUTPUT_CHANNELS // PRUNE_CHANNELS), 0, 4) < 3).astype(jnp.int32), jax.random.fold_in(key_of[4], 1), 0, 1)
    pointwise_prune_mask = place_ends((jax.random.randint(key_of[5], (RESIDUAL_COUNT, OUTPUT_CHANNELS, OUTPUT_CHANNELS // PRUNE_CHANNELS), 0, 4) < 3).astype(jnp.int32), jax.random.fold_in(key_of[5], 1), 0, 1)
    snake_freq_upsample = jnp.clip(jnp.exp(math.log(3.0) - 1.7917595 * jax.random.uniform(key_of[6], (D_IN,), jnp.float32) ** levels(key_of[6], (D_IN,), ((0, 8),), -0.2, 0.2)), 0.5, 3.0)
    snake_freq_dilated = jnp.clip(jnp.exp(math.log(3.0) - 1.7917595 * jax.random.uniform(key_of[7], (RESIDUAL_COUNT, OUTPUT_CHANNELS), jnp.float32) ** levels(key_of[7], (RESIDUAL_COUNT, OUTPUT_CHANNELS), ((1, 8),), -0.2, 0.2)), 0.5, 3.0)
    snake_freq_pointwise = jnp.clip(jnp.exp(math.log(3.0) - 1.7917595 * jax.random.uniform(key_of[8], (RESIDUAL_COUNT, OUTPUT_CHANNELS), jnp.float32) ** levels(key_of[8], (RESIDUAL_COUNT, OUTPUT_CHANNELS), ((1, 8),), -0.2, 0.2)), 0.5, 3.0)
    segment_lengths = draw_segment_lengths(jax.random.fold_in(key_of[11], 71), 0)
    cotangent = noise(key_of[10], (OUTPUT_CHANNELS, ROWS), 1.0, 6.0, ((0, 8), (1, 4)))
    return {"latent_input": latent_input, "upsample_kernel": upsample_kernel, "dilated_kernel": dilated_kernel, "pointwise_kernel": pointwise_kernel, "dilated_prune_mask": dilated_prune_mask, "pointwise_prune_mask": pointwise_prune_mask, "snake_freq_upsample": snake_freq_upsample, "snake_freq_dilated": snake_freq_dilated, "snake_freq_pointwise": snake_freq_pointwise, "segment_lengths": segment_lengths, "cotangent": cotangent}


def snake_act(values, alpha):
    scale = alpha[:, None]
    return values + jnp.sin(scale * values) ** 2 / scale


def snake_slope(values, alpha):
    return 1.0 + jnp.sin(2.0 * alpha[:, None] * values)


def track_ids(lengths, frame_index, total_frames):
    starts = jnp.cumsum(lengths) - lengths
    found = jnp.sum((starts[:, None] <= frame_index[None, :]).astype(jnp.int32), axis=0) - 1
    return jnp.where(frame_index < 0, -1, jnp.where(frame_index >= total_frames, -2, found)).astype(jnp.int32)


def rounded_groups(grouped_weight_sums, grad_groups, contract):
    def step_fn(totals, inputs):
        weight_part, grad_part = inputs
        partial_sum = lax.dot_general(weight_part, grad_part, ((contract, contract), ((), ())), preferred_element_type=jnp.float32)
        narrow = lax.optimization_barrier(partial_sum.astype(jnp.bfloat16))
        return totals + narrow.astype(jnp.float32), None

    start_sum = jnp.zeros((grouped_weight_sums.shape[-1], grad_groups.shape[-1]), jnp.float32)
    result, unused = lax.scan(step_fn, start_sum, (grouped_weight_sums, grad_groups))
    return result


def reference(latent_input, upsample_kernel, dilated_kernel, pointwise_kernel, dilated_prune_mask, pointwise_prune_mask, snake_freq_upsample, snake_freq_dilated, snake_freq_pointwise, segment_lengths, cotangent):
    half_stride = STRIDE // 2
    channel_group_width = OUTPUT_CHANNELS // N_CHAN
    frame_pos = jnp.arange(FRAMES, dtype=jnp.int32)
    activated = snake_act(latent_input.astype(jnp.float32), snake_freq_upsample).astype(jnp.bfloat16)
    frame_ids = track_ids(segment_lengths, frame_pos, FRAMES)
    prev_ok = (frame_ids == track_ids(segment_lengths, frame_pos - 1, FRAMES)).astype(jnp.float32)
    next_ok = (frame_ids == track_ids(segment_lengths, frame_pos + 1, FRAMES)).astype(jnp.float32)
    zero_column = jnp.zeros((D_IN, 1), jnp.bfloat16)
    earlier = jnp.concatenate([zero_column, activated[:, :-1]], axis=1)
    later = jnp.concatenate([activated[:, 1:], zero_column], axis=1)
    outputs = []
    for phase_index in range(STRIDE):
        middle = jnp.dot(upsample_kernel[phase_index + half_stride], activated, preferred_element_type=jnp.float32)
        if phase_index < half_stride:
            neighbour = jnp.dot(upsample_kernel[phase_index + half_stride + STRIDE], earlier, preferred_element_type=jnp.float32) * prev_ok[None, :]
        else:
            neighbour = jnp.dot(upsample_kernel[phase_index - half_stride], later, preferred_element_type=jnp.float32) * next_ok[None, :]
        outputs.append(middle + neighbour)
    hidden_state = jnp.stack(outputs, axis=-1).reshape(OUTPUT_CHANNELS, ROWS)

    row_pos = jnp.arange(ROWS, dtype=jnp.int32)
    own_ids = track_ids(segment_lengths, jnp.floor_divide(row_pos, STRIDE), FRAMES)

    def tap_mask(offset):
        other = track_ids(segment_lengths, jnp.floor_divide(row_pos + offset, STRIDE), FRAMES)
        return (own_ids == other).astype(jnp.float32)

    saved_residuals = []
    for residual_unit_index in range(RESIDUAL_COUNT):
        spacing = 3 ** (residual_unit_index + 1)
        margin = 3 * spacing
        dilated_effective = dilated_kernel[residual_unit_index] * jnp.repeat(dilated_prune_mask[residual_unit_index], PRUNE_CHANNELS, axis=-1).astype(jnp.bfloat16)
        pointwise_effective = pointwise_kernel[residual_unit_index] * jnp.repeat(pointwise_prune_mask[residual_unit_index], PRUNE_CHANNELS, axis=-1).astype(jnp.bfloat16)
        first = snake_act(hidden_state, snake_freq_dilated[residual_unit_index]).astype(jnp.bfloat16)
        padded_input = jnp.pad(first, ((0, 0), (margin, margin)))
        kernel_tap_masks = jnp.stack([tap_mask((kernel_tap_index - 3) * spacing) for kernel_tap_index in range(DILATED_TAPS)])
        conv_result = jnp.zeros((OUTPUT_CHANNELS, ROWS), jnp.float32)
        for kernel_tap_index in range(DILATED_TAPS):
            track_window = padded_input[:, kernel_tap_index * spacing:kernel_tap_index * spacing + ROWS]
            conv_result = conv_result + kernel_tap_masks[kernel_tap_index][None, :] * jnp.dot(dilated_effective[kernel_tap_index], track_window, preferred_element_type=jnp.float32)
        second_activation = snake_act(conv_result, snake_freq_pointwise[residual_unit_index]).astype(jnp.bfloat16)
        saved_residuals.append((hidden_state, padded_input, kernel_tap_masks, conv_result, second_activation, dilated_effective, pointwise_effective))
        hidden_state = hidden_state + jnp.dot(pointwise_effective, second_activation, preferred_element_type=jnp.float32)
    decoded = hidden_state.astype(jnp.bfloat16)

    grad_out = cotangent.astype(jnp.float32)
    dilated_weight_list = [None] * RESIDUAL_COUNT
    pointwise_weight_list = [None] * RESIDUAL_COUNT
    for residual_unit_index in reversed(range(RESIDUAL_COUNT)):
        spacing = 3 ** (residual_unit_index + 1)
        margin = 3 * spacing
        hidden_input, padded_input, kernel_tap_masks, conv_result, second_activation, dilated_effective, pointwise_effective = saved_residuals[residual_unit_index]
        grad_b = grad_out.astype(jnp.bfloat16)
        pointwise_gradient = lax.dot_general(grad_b, second_activation, (((1,), (1,)), ((), ())), preferred_element_type=jnp.float32)
        grad_second = rounded_groups(pointwise_effective.reshape(N_CHAN, channel_group_width, OUTPUT_CHANNELS), grad_b.reshape(N_CHAN, channel_group_width, ROWS), (0,))
        grad_conv = (grad_second * snake_slope(conv_result, snake_freq_pointwise[residual_unit_index])).astype(jnp.bfloat16)
        masked_kernel = grad_conv[None, :, :] * kernel_tap_masks[:, None, :].astype(jnp.bfloat16)
        track_window_list = jnp.stack([padded_input[:, kernel_tap_index * spacing:kernel_tap_index * spacing + ROWS] for kernel_tap_index in range(DILATED_TAPS)])
        dilated_gradient = jnp.einsum("jdo,jso->jds", masked_kernel.astype(jnp.float32), track_window_list.astype(jnp.float32))
        dilated_weight_list[residual_unit_index] = dilated_effective.astype(jnp.float32) * dilated_gradient
        pointwise_weight_list[residual_unit_index] = pointwise_effective.astype(jnp.float32) * pointwise_gradient
        if residual_unit_index > 0:
            shifted_pad = jnp.pad(masked_kernel, ((0, 0), (0, 0), (margin, margin)))
            shifted = jnp.stack([shifted_pad[kernel_tap_index, :, (6 - kernel_tap_index) * spacing:(6 - kernel_tap_index) * spacing + ROWS] for kernel_tap_index in range(DILATED_TAPS)])
            grouped_weight_sums = dilated_effective.reshape(DILATED_TAPS, N_CHAN, channel_group_width, OUTPUT_CHANNELS).transpose(1, 0, 2, 3)
            grad_groups = shifted.reshape(DILATED_TAPS, N_CHAN, channel_group_width, ROWS).transpose(1, 0, 2, 3)
            grad_first = rounded_groups(grouped_weight_sums, grad_groups, (0, 1))
            grad_out = grad_out + grad_first * snake_slope(hidden_input, snake_freq_dilated[residual_unit_index])
    return decoded, jnp.stack(dilated_weight_list), jnp.stack(pointwise_weight_list)
```

```python
import functools

import jax
import jax.numpy as jnp
from jax import lax
from jax.experimental import pallas as pl
from jax.experimental.pallas import tpu as pltpu
from jax.sharding import PartitionSpec as P

MESH = pl.DeviceIdType.MESH
BF16 = jnp.bfloat16
F32 = jnp.float32
VMEM_LIMIT = 48 * 1024 * 1024


def remote(src, dst, send, recv, device):
    return pltpu.make_async_remote_copy(
        src_ref=src, dst_ref=dst, send_sem=send, recv_sem=recv, device_id=device, device_id_type=MESH
    )


def greet(devices):
    barrier = pltpu.get_barrier_semaphore()
    for device in devices:
        pl.semaphore_signal(barrier, inc=1, device_id=device, device_id_type=MESH)
    pl.semaphore_wait(barrier, len(devices))


def chan_place():
    tm, chan = lax.axis_index("tm"), lax.axis_index("chan")
    chips = lax.axis_size("chan") // 2
    chip, core = chan // 2, chan % 2
    partner = (tm, chan + 1 - 2 * core)

    def at(step):
        return ((chip + step + chips) % chips) * 2 + core

    return tm, chan, core, chips, partner, at


def column(index, width):
    return pl.ds(pl.multiple_of(index * width, width), width)


def chan_gather_kernel(halo, x_ref, o_ref, send, recv, fsend, frecv, hsend, hrecv):
    tm, chan, core, chips, partner, at = chan_place()
    frames = lax.axis_size("tm")
    rows, width = x_ref.shape
    greeted = [partner] + [(tm, at(step)) for step in range(1, chips)]
    after = ((tm + 1) % frames, chan)
    before = ((tm + frames - 1) % frames, chan)
    if halo:
        greeted += [before, after]
    greet(greeted)
    spans = [pl.ds(halo, rows)]
    sources = [x_ref]
    mine = column(chan, width)
    if halo:
        spans += [pl.ds(0, halo), pl.ds(halo + rows, halo)]
        sources += [o_ref.at[spans[1], mine], o_ref.at[spans[2], mine]]
        edges = [
            remote(x_ref.at[pl.ds(rows - halo, halo)], o_ref.at[spans[1], mine], hsend.at[0], hrecv.at[0], after),
            remote(x_ref.at[pl.ds(0, halo)], o_ref.at[spans[2], mine], hsend.at[1], hrecv.at[1], before),
        ]
        for edge in edges:
            edge.start()
    started = []

    def spread(part):
        for step in range(1, chips):
            copy = remote(
                sources[part], o_ref.at[spans[part], mine], send.at[part, step], recv.at[part, step], (tm, at(step))
            )
            copy.start()
            started.append(copy)
        copy = remote(sources[part], o_ref.at[spans[part], mine], send.at[part, 0], recv.at[part, 0], partner)
        copy.start()
        started.append(copy)

    spread(0)
    if halo:
        for edge in edges:
            edge.wait_recv()
        spread(1)
        spread(2)
    o_ref[spans[0], mine] = x_ref[...]

    def arrival(part, index, sems, step):
        slot = o_ref.at[spans[part], column(index, width)]
        return remote(slot, slot, send.at[part, step], sems.at[part, step], partner)

    for step in range(1, chips):
        for part in range(len(spans)):
            index = at(-step)
            arrival(part, index, recv, step).wait_recv()
            slot = o_ref.at[spans[part], column(index, width)]
            copy = remote(slot, slot, fsend.at[part, step], frecv.at[part, step], partner)
            copy.start()
            started.append(copy)
    other = 1 - 2 * core
    for part in range(len(spans)):
        arrival(part, chan + other, recv, 0).wait_recv()
        for step in range(1, chips):
            arrival(part, at(-step) + other, frecv, step).wait_recv()
    for copy in started:
        copy.wait_send()
    if halo:
        for edge in edges:
            edge.wait_send()


def chan_scatter_kernel(x_ref, o_ref, pair, summed, landed, psend, precv, send, recv):
    tm, chan, core, chips, partner, at = chan_place()
    width = o_ref.shape[1]
    greet([partner] + [(tm, at(step)) for step in range(1, chips)])
    other = 1 - 2 * core
    order = list(range(1, chips)) + [0]
    started = []
    pairs = {}
    for step in order:
        copy = remote(
            x_ref.at[:, column(at(step) + other, width)], pair.at[step], psend.at[step], precv.at[step], partner
        )
        copy.start()
        pairs[step] = copy
    for step in range(1, chips):
        pairs[step].wait_recv()
        summed[step] = (
            x_ref[:, column(at(step), width)].astype(F32) + pair[step].astype(F32)
        ).astype(summed.dtype)
        copy = remote(summed.at[step], landed.at[step], send.at[step], recv.at[step], (tm, at(step)))
        copy.start()
        started.append(copy)
    pairs[0].wait_recv()
    o_ref[...] = x_ref[:, column(chan, width)].astype(F32) + pair[0].astype(F32)
    for copy, step in zip(started, range(1, chips)):
        copy.wait_recv()
        o_ref[...] += landed[step].astype(F32)
    for copy in started:
        copy.wait_send()
    for step in order:
        pairs[step].wait_send()


def tm_scatter_kernel(x_ref, o_ref, landed, send, recv):
    tm, chan = lax.axis_index("tm"), lax.axis_index("chan")
    count = lax.axis_size("tm")
    rows = o_ref.shape[0]
    greet([((tm + step) % count, chan) for step in range(1, count)])
    started = []
    for step in range(1, count):
        to = (tm + step) % count
        copy = remote(
            x_ref.at[pl.ds(pl.multiple_of(to * rows, rows), rows)],
            landed.at[step],
            send.at[step],
            recv.at[step],
            (to, chan),
        )
        copy.start()
        started.append(copy)
    o_ref[...] = x_ref[pl.ds(pl.multiple_of(tm * rows, rows), rows)].astype(F32)
    for step in range(1, count):
        started[step - 1].wait_recv()
        o_ref[...] += landed[step].astype(F32)
    for copy in started:
        copy.wait_send()


def tm_gather_kernel(x_ref, o_ref, send, recv):
    tm, chan = lax.axis_index("tm"), lax.axis_index("chan")
    count = lax.axis_size("tm")
    rows = x_ref.shape[0]
    greet([((tm + step) % count, chan) for step in range(1, count)])

    def slot(index):
        return o_ref.at[pl.ds(pl.multiple_of(index * rows, rows), rows)]

    started = []
    for step in range(1, count):
        copy = remote(x_ref, slot(tm), send.at[step], recv.at[step], ((tm + step) % count, chan))
        copy.start()
        started.append(copy)
    o_ref[pl.ds(pl.multiple_of(tm * rows, rows), rows)] = x_ref[...]
    for step in range(1, count):
        landing = slot((tm + count - step) % count)
        remote(landing, landing, send.at[step], recv.at[step], (tm, chan)).wait_recv()
    for copy in started:
        copy.wait_send()


def turn_kernel(x_ref, o_ref, send, recv):
    tm, chan = lax.axis_index("tm"), lax.axis_index("chan")
    frames, chans = lax.axis_size("tm"), lax.axis_size("chan")
    ratio = chans // frames
    rows, width = x_ref.shape
    target = chan // ratio
    own = target == tm
    barrier = pltpu.get_barrier_semaphore()
    for frame in range(frames):
        for part in range(ratio):
            source = (frame, tm * ratio + part)

            @pl.when(jnp.logical_or(frame != tm, source[1] != chan))
            def _():
                pl.semaphore_signal(barrier, inc=1, device_id=source, device_id_type=MESH)

    @pl.when(own)
    def _():
        pl.semaphore_wait(barrier, chans - 1)

    @pl.when(jnp.logical_not(own))
    def _():
        pl.semaphore_wait(barrier, chans)

    slot_rows = pl.ds(pl.multiple_of(tm * rows, rows), rows)
    slot_columns = column(chan % ratio, width)
    which = tm * ratio + chan % ratio

    def outgoing(step):
        return remote(
            x_ref,
            o_ref.at[slot_rows, slot_columns],
            send.at[step],
            recv.at[which],
            (target, (chan + step) % chans),
        )

    for step in range(1, chans):
        outgoing(step).start()

    @pl.when(own)
    def _():
        o_ref[slot_rows, slot_columns] = x_ref[...]

    @pl.when(jnp.logical_not(own))
    def _():
        outgoing(0).start()

    for frame in range(frames):
        for part in range(ratio):

            @pl.when(jnp.logical_or(frame != tm, tm * ratio + part != chan))
            def _():
                landing = o_ref.at[pl.ds(frame * rows, rows), pl.ds(part * width, width)]
                remote(
                    landing, landing, send.at[0], recv.at[frame * ratio + part], (tm, chan)
                ).wait_recv()

    for step in range(1, chans):
        outgoing(step).wait_send()

    @pl.when(jnp.logical_not(own))
    def _():
        outgoing(0).wait_send()


def run(kernel, out_shape, dtype, scratch, number, value):
    whole = pl.BlockSpec(memory_space=pltpu.VMEM)
    return pl.pallas_call(
        kernel,
        out_shape=jax.ShapeDtypeStruct(out_shape, dtype),
        in_specs=[whole],
        out_specs=whole,
        scratch_shapes=scratch,
        compiler_params=pltpu.CompilerParams(
            collective_id=number, has_side_effects=True, vmem_limit_bytes=VMEM_LIMIT
        ),
    )(value)


def plain_kernels(*widths):
    return all(width % 128 == 0 for width in widths)


def with_halo(cells, width):
    count = lax.axis_size("tm")
    head, tail = cells[:width], cells[-width:]
    return jnp.concatenate(
        [
            lax.ppermute(tail, "tm", [(i, (i + 1) % count) for i in range(count)]),
            cells,
            lax.ppermute(head, "tm", [((i + 1) % count, i) for i in range(count)]),
        ],
        axis=0,
    )


def chan_gather(value, halo, number):
    rows, width = value.shape
    chans = lax.axis_size("chan")
    if not plain_kernels(width):
        return lax.all_gather(with_halo(value, halo) if halo else value, "chan", axis=1, tiled=True)
    chips = chans // 2
    dma = pltpu.SemaphoreType.DMA
    return run(
        functools.partial(chan_gather_kernel, halo),
        (rows + 2 * halo, width * chans),
        value.dtype,
        [dma((3, chips))] * 4 + [dma((2,))] * 2,
        number,
        value,
    )


def chan_scatter(value, number):
    rows, total = value.shape
    chans = lax.axis_size("chan")
    width = total // chans
    if not plain_kernels(width):
        return lax.psum_scatter(value, "chan", scatter_dimension=1, tiled=True).astype(F32)
    chips = chans // 2
    dma = pltpu.SemaphoreType.DMA
    return run(
        chan_scatter_kernel,
        (rows, width),
        F32,
        [pltpu.VMEM((chips, rows, width), value.dtype)] * 3 + [dma((chips,))] * 4,
        number,
        value,
    )


def tm_scatter(value, number):
    count = lax.axis_size("tm")
    rows, width = value.shape[0] // count, value.shape[1]
    if not plain_kernels(width):
        return lax.psum_scatter(value, "tm", scatter_dimension=0, tiled=True).astype(F32)
    dma = pltpu.SemaphoreType.DMA
    return run(
        tm_scatter_kernel,
        (rows, width),
        F32,
        [pltpu.VMEM((count, rows, width), value.dtype)] + [dma((count,))] * 2,
        number,
        value,
    )


def tm_gather(value, number):
    count = lax.axis_size("tm")
    rows, width = value.shape
    if not plain_kernels(width):
        return lax.all_gather(value, "tm", axis=0, tiled=True)
    return run(
        tm_gather_kernel, (rows * count, width), value.dtype, [pltpu.SemaphoreType.DMA((count,))] * 2, number, value
    )


def turn(value, number):
    frames, chans = lax.axis_size("tm"), lax.axis_size("chan")
    rows, width = value.shape
    if not plain_kernels(width) or chans % frames:
        return lax.all_to_all(
            lax.all_gather(value, "chan", axis=1, tiled=True), "tm", split_axis=1, concat_axis=0, tiled=True
        )
    return run(
        turn_kernel,
        (rows * frames, width * chans // frames),
        value.dtype,
        [pltpu.SemaphoreType.DMA((chans,))] * 2,
        number,
        value,
    )


def snake_act(values, alpha):
    return values + jnp.sin(alpha * values) ** 2 / alpha


def snake_slope(values, alpha):
    return 1.0 + jnp.sin(2.0 * alpha * values)


def track_ids(lengths, frame_index, total_frames):
    starts = jnp.cumsum(lengths) - lengths
    found = jnp.sum((starts[:, None] <= frame_index[None, :]).astype(jnp.int32), axis=0) - 1
    return jnp.where(frame_index < 0, -1, jnp.where(frame_index >= total_frames, -2, found))


def dot_last(left, right):
    return lax.dot_general(left, right, (((1,), (1,)), ((), ())), preferred_element_type=F32)


def dot_first(left, right):
    return lax.dot_general(left, right, (((0,), (0,)), ((), ())), preferred_element_type=F32)


def expand(kernel, mask):
    width, blocks = kernel.shape[-1], mask.shape[-1]
    spread = (
        jnp.arange(width, dtype=jnp.int32)[None, :] // (width // blocks)
        == jnp.arange(blocks, dtype=jnp.int32)[:, None]
    ).astype(BF16)
    keep = jnp.dot(mask.reshape(-1, blocks).astype(BF16), spread, preferred_element_type=F32)
    return (kernel.reshape(-1, width) * keep.astype(BF16)).reshape(kernel.shape)


def per_device(
    latent_input,
    upsample_kernel,
    dilated_kernel,
    pointwise_kernel,
    dilated_prune_mask,
    pointwise_prune_mask,
    snake_freq_upsample,
    snake_freq_dilated,
    snake_freq_pointwise,
    segment_lengths,
    cotangent,
):
    taps, out_local, in_local = upsample_kernel.shape
    stride = taps // 2
    half = stride // 2
    frame_count = latent_input.shape[1]
    rows = frame_count * stride
    tm_count = lax.axis_size("tm")
    tm_index = lax.axis_index("tm")
    total_frames = frame_count * tm_count
    units, kernel_taps, _, channels = dilated_kernel.shape

    def tap_mask(pos, offset):
        own = track_ids(segment_lengths, jnp.floor_divide(pos, stride), total_frames)
        other = track_ids(segment_lengths, jnp.floor_divide(pos + offset, stride), total_frames)
        return (own == other)[:, None]

    row_pos = tm_index * rows + jnp.arange(rows, dtype=jnp.int32)
    all_pos = jnp.arange(rows * tm_count, dtype=jnp.int32)
    frame_pos = jnp.arange(total_frames, dtype=jnp.int32)

    dil_eff = expand(dilated_kernel, dilated_prune_mask)
    point_eff = expand(pointwise_kernel, pointwise_prune_mask)

    act = snake_act(latent_input.astype(F32), snake_freq_upsample[:, None]).astype(BF16).T
    cot = cotangent.T
    grad_second_last = lax.psum_scatter(
        jnp.dot(cot, point_eff[units - 1], preferred_element_type=F32).astype(BF16),
        "chan",
        scatter_dimension=1,
        tiled=True,
    ).astype(F32)

    act_all = turn(act, 0)
    product = dot_last(act_all, upsample_kernel.reshape(taps * out_local, in_local)).reshape(
        total_frames, taps, out_local
    )
    frame_ids = track_ids(segment_lengths, frame_pos, total_frames)
    prev_ok = (frame_ids == track_ids(segment_lengths, frame_pos - 1, total_frames))[:, None, None]
    next_ok = (frame_ids == track_ids(segment_lengths, frame_pos + 1, total_frames))[:, None, None]
    low = jnp.pad(product[:-1, half + stride :], ((1, 0), (0, 0), (0, 0)))
    high = jnp.pad(product[1:, :half], ((0, 1), (0, 0), (0, 0)))
    partial = product[:, half : half + stride] + jnp.concatenate(
        [jnp.where(prev_ok, low, 0.0), jnp.where(next_ok, high, 0.0)], axis=1
    )
    hidden = tm_scatter(partial.astype(BF16).reshape(rows * tm_count, out_local), 1)

    saved = []
    number = 2
    for unit in range(units):
        spacing = 3 ** (unit + 1)
        margin = (kernel_taps // 2) * spacing
        halo = -(-margin // 16) * 16
        first = snake_act(hidden, snake_freq_dilated[unit]).astype(BF16)
        first_all = chan_gather(first, halo, number)
        number += 1
        spans = dot_last(first_all, dil_eff[unit].reshape(kernel_taps * out_local, channels))
        conv = jnp.zeros((rows, out_local), F32)
        for tap in range(kernel_taps):
            shift = (tap - kernel_taps // 2) * spacing
            piece = spans[halo + shift : halo + shift + rows, tap * out_local : (tap + 1) * out_local]
            conv = conv + jnp.where(tap_mask(row_pos, shift), piece, 0.0)
        second = snake_act(conv, snake_freq_pointwise[unit]).astype(BF16)
        if unit < units - 1:
            second_all = chan_gather(second, 0, number)
            number += 1
        else:
            second_all = lax.all_gather(second, "chan", axis=1, tiled=True)
        saved.append((hidden, first_all[halo : halo + rows], conv, second_all))
        hidden = hidden + dot_last(second_all, point_eff[unit])
    decoded = hidden.astype(BF16).T

    first_frames = lax.all_gather(saved[0][1], "tm", axis=0, tiled=True)

    def shifted_taps(grad_wide, pos, halo, spacing):
        count = pos.shape[0]
        pieces = []
        for tap in range(kernel_taps):
            shift = (tap - kernel_taps // 2) * spacing
            window = grad_wide[halo - shift : halo - shift + count]
            pieces.append(jnp.where(tap_mask(pos, -shift), window, jnp.zeros((), BF16)))
        return jnp.concatenate(pieces, axis=1)

    grad_out = cot.astype(F32)
    dil_out = [None] * units
    point_out = [None] * units
    for unit in reversed(range(units)):
        spacing = 3 ** (unit + 1)
        margin = (kernel_taps // 2) * spacing
        hidden_in, first_own, conv, second_all = saved[unit]
        grad_b = grad_out.astype(BF16)
        point_grad = dot_first(grad_b, second_all)
        if unit == units - 1:
            grad_second = grad_second_last
        else:
            grad_second = chan_scatter(
                jnp.dot(grad_b, point_eff[unit], preferred_element_type=F32).astype(BF16), number
            )
            number += 1
        grad_conv = (grad_second * snake_slope(conv, snake_freq_pointwise[unit])).astype(BF16)
        weights = dil_eff[unit].reshape(kernel_taps * out_local, channels)
        if unit > 0:
            shifted = shifted_taps(with_halo(grad_conv, margin), row_pos, margin, spacing)
            grad_first = chan_scatter(
                jnp.dot(shifted, weights, preferred_element_type=F32).astype(BF16), number
            )
            number += 1
            dil_part, point_part = lax.psum(
                (dot_first(shifted, first_own).astype(BF16), point_grad.astype(BF16)), "tm"
            )
            dil_grad = dil_part.astype(F32)
            grad_out = grad_out + grad_first * snake_slope(hidden_in, snake_freq_dilated[unit])
        else:
            grad_frames = jnp.pad(tm_gather(grad_conv, number), ((margin, margin), (0, 0)))
            number += 1
            dil_grad = dot_first(shifted_taps(grad_frames, all_pos, margin, spacing), first_frames)
            point_part = lax.psum(point_grad.astype(BF16), "tm")
        dil_out[unit] = (weights.astype(F32) * dil_grad).reshape(kernel_taps, out_local, channels)
        point_out[unit] = point_eff[unit].astype(F32) * point_part.astype(F32)
    return decoded, jnp.stack(dil_out), jnp.stack(point_out)


def solution(mesh):
    return jax.shard_map(
        per_device,
        mesh=mesh,
        in_specs=(
            P("chan", "tm"),
            P(None, "chan", "tm"),
            P(None, None, "chan", None),
            P(None, "chan", None),
            P(None, None, "chan", None),
            P(None, "chan", None),
            P("chan"),
            P(None, "chan"),
            P(None, "chan"),
            P(),
            P("chan", "tm"),
        ),
        out_specs=(P("chan", "tm"), P(None, None, "chan", None), P(None, "chan", None)),
        check_vma=False,
    )
```

```python
import functools

import jax
import jax.numpy as jnp
from jax import lax
from jax.experimental import pallas as pl
from jax.experimental.pallas import tpu as pltpu
from jax.sharding import PartitionSpec as P

MESH = pl.DeviceIdType.MESH
BF16 = jnp.bfloat16
F32 = jnp.float32
VMEM_LIMIT = 48 * 1024 * 1024


def remote(src, dst, send, recv, device):
    return pltpu.make_async_remote_copy(
        src_ref=src, dst_ref=dst, send_sem=send, recv_sem=recv, device_id=device, device_id_type=MESH
    )


def greet(devices):
    barrier = pltpu.get_barrier_semaphore()
    for device in devices:
        pl.semaphore_signal(barrier, inc=1, device_id=device, device_id_type=MESH)
    pl.semaphore_wait(barrier, len(devices))


def chan_place():
    tm, chan = lax.axis_index("tm"), lax.axis_index("chan")
    chips = lax.axis_size("chan") // 2
    chip, core = chan // 2, chan % 2
    partner = (tm, chan + 1 - 2 * core)

    def at(step):
        return ((chip + step + chips) % chips) * 2 + core

    return tm, chan, core, chips, partner, at


def column(index, width):
    return pl.ds(pl.multiple_of(index * width, width), width)


def chan_gather_task(halo):
    def body(x_ref, o_ref, send, recv, fsend, frecv, hsend, hrecv):
        tm, chan, core, chips, partner, at = chan_place()
        frames = lax.axis_size("tm")
        rows, width = x_ref.shape
        after = ((tm + 1) % frames, chan)
        before = ((tm + frames - 1) % frames, chan)
        spans = [pl.ds(halo, rows)]
        sources = [x_ref]
        mine = column(chan, width)
        if halo:
            spans += [pl.ds(0, halo), pl.ds(halo + rows, halo)]
            sources += [o_ref.at[spans[1], mine], o_ref.at[spans[2], mine]]
            edges = [
                remote(x_ref.at[pl.ds(rows - halo, halo)], o_ref.at[spans[1], mine], hsend.at[0], hrecv.at[0], after),
                remote(x_ref.at[pl.ds(0, halo)], o_ref.at[spans[2], mine], hsend.at[1], hrecv.at[1], before),
            ]
            for edge in edges:
                edge.start()
        started = []

        def spread(part):
            for step in range(1, chips):
                copy = remote(
                    sources[part], o_ref.at[spans[part], mine], send.at[part, step], recv.at[part, step], (tm, at(step))
                )
                copy.start()
                started.append(copy)
            copy = remote(sources[part], o_ref.at[spans[part], mine], send.at[part, 0], recv.at[part, 0], partner)
            copy.start()
            started.append(copy)

        spread(0)
        yield
        if halo:
            for edge in edges:
                edge.wait_recv()
            spread(1)
            spread(2)
        o_ref[spans[0], mine] = x_ref[...]

        def arrival(part, index, sems, step):
            slot = o_ref.at[spans[part], column(index, width)]
            return remote(slot, slot, send.at[part, step], sems.at[part, step], partner)

        for step in range(1, chips):
            for part in range(len(spans)):
                index = at(-step)
                arrival(part, index, recv, step).wait_recv()
                slot = o_ref.at[spans[part], column(index, width)]
                copy = remote(slot, slot, fsend.at[part, step], frecv.at[part, step], partner)
                copy.start()
                started.append(copy)
        yield
        other = 1 - 2 * core
        for part in range(len(spans)):
            arrival(part, chan + other, recv, 0).wait_recv()
            for step in range(1, chips):
                arrival(part, at(-step) + other, frecv, step).wait_recv()
        for copy in started:
            copy.wait_send()
        if halo:
            for edge in edges:
                edge.wait_send()

    return body


def chan_scatter_body(x_ref, o_ref, pair, summed, landed, psend, precv, send, recv):
    tm, chan, core, chips, partner, at = chan_place()
    width = o_ref.shape[1]
    other = 1 - 2 * core
    order = list(range(1, chips)) + [0]
    started = []
    pairs = {}
    for step in order:
        copy = remote(
            x_ref.at[:, column(at(step) + other, width)], pair.at[step], psend.at[step], precv.at[step], partner
        )
        copy.start()
        pairs[step] = copy
    yield
    for step in range(1, chips):
        pairs[step].wait_recv()
        summed[step] = (
            x_ref[:, column(at(step), width)].astype(F32) + pair[step].astype(F32)
        ).astype(summed.dtype)
        copy = remote(summed.at[step], landed.at[step], send.at[step], recv.at[step], (tm, at(step)))
        copy.start()
        started.append(copy)
    pairs[0].wait_recv()
    o_ref[...] = x_ref[:, column(chan, width)].astype(F32) + pair[0].astype(F32)
    yield
    for copy, step in zip(started, range(1, chips)):
        copy.wait_recv()
        o_ref[...] += landed[step].astype(F32)
    for copy in started:
        copy.wait_send()
    for step in order:
        pairs[step].wait_send()


def share_task(halo, base):
    def body(x_ref, o_ref, send, recv, fsend, frecv):
        tm, chan, core, chips, partner, at = chan_place()
        count = lax.axis_size("tm")
        rows, width = o_ref.shape[0] // count, o_ref.shape[1] // 2
        own = pl.ds(halo, rows)

        def slot(index, half):
            return o_ref.at[pl.ds(pl.multiple_of(index * rows, rows), rows), column(half, width)]

        started = []
        source = x_ref.at[own, pl.ds(pl.multiple_of(base + core * width, width), width)]
        for step in range(1, count):
            copy = remote(source, slot(tm, core), send.at[step], recv.at[step], ((tm + step) % count, chan))
            copy.start()
            started.append(copy)
        yield
        o_ref[pl.ds(pl.multiple_of(tm * rows, rows), rows), :] = x_ref[own, pl.ds(base, 2 * width)]
        for step in range(1, count):
            landing = slot((tm + count - step) % count, core)
            remote(landing, landing, send.at[step], recv.at[step], partner).wait_recv()
            copy = remote(landing, landing, fsend.at[step], frecv.at[step], partner)
            copy.start()
            started.append(copy)
        yield
        for step in range(1, count):
            landing = slot((tm + count - step) % count, 1 - core)
            remote(landing, landing, send.at[step], frecv.at[step], partner).wait_recv()
        for copy in started:
            copy.wait_send()

    return body


def frames_gather_body(x_ref, o_ref, send, recv):
    tm, chan = lax.axis_index("tm"), lax.axis_index("chan")
    count = lax.axis_size("tm")
    rows = x_ref.shape[0]

    def slot(index):
        return o_ref.at[pl.ds(pl.multiple_of(index * rows, rows), rows)]

    started = []
    for step in range(1, count):
        copy = remote(x_ref, slot(tm), send.at[step], recv.at[step], ((tm + step) % count, chan))
        copy.start()
        started.append(copy)
    yield
    o_ref[pl.ds(pl.multiple_of(tm * rows, rows), rows)] = x_ref[...]
    yield
    for step in range(1, count):
        landing = slot((tm + count - step) % count)
        remote(landing, landing, send.at[step], recv.at[step], (tm, chan)).wait_recv()
    for copy in started:
        copy.wait_send()


def reduce_body(x_ref, o_ref, landed, send, recv, gsend, grecv):
    tm, chan = lax.axis_index("tm"), lax.axis_index("chan")
    count = lax.axis_size("tm")
    width = x_ref.shape[1] // count
    started = []
    for step in range(1, count):
        to = (tm + step) % count
        copy = remote(x_ref.at[:, column(to, width)], landed.at[step], send.at[step], recv.at[step], (to, chan))
        copy.start()
        started.append(copy)
    yield
    total = x_ref[:, column(tm, width)].astype(F32)
    for step in range(1, count):
        started[step - 1].wait_recv()
        total += landed[step].astype(F32)
    mine = o_ref.at[:, column(tm, width)]
    o_ref[:, column(tm, width)] = total.astype(o_ref.dtype)
    for step in range(1, count):
        copy = remote(mine, mine, gsend.at[step], grecv.at[step], ((tm + step) % count, chan))
        copy.start()
        started.append(copy)
    yield
    for step in range(1, count):
        landing = o_ref.at[:, column((tm + count - step) % count, width)]
        remote(landing, landing, send.at[step], grecv.at[step], (tm, chan)).wait_recv()
    for copy in started:
        copy.wait_send()


DMA = pltpu.SemaphoreType.DMA


def chan_gather(value, halo):
    rows, width = value.shape
    chans = lax.axis_size("chan")
    out = jax.ShapeDtypeStruct((rows + 2 * halo, width * chans), value.dtype)
    return value, out, [DMA((3, chans // 2))] * 4 + [DMA((2,))] * 2, chan_gather_task(halo), False, halo > 0


def chan_scatter(value):
    rows, chans = value.shape[0], lax.axis_size("chan")
    width, chips = value.shape[1] // chans, chans // 2
    scratch = [pltpu.VMEM((chips, rows, width), value.dtype)] * 3 + [DMA((chips,))] * 4
    return value, jax.ShapeDtypeStruct((rows, width), F32), scratch, chan_scatter_body, False, False


def share(value, halo, part, parts):
    count = lax.axis_size("tm")
    rows, width = value.shape[0] - 2 * halo, value.shape[1] // parts
    out = jax.ShapeDtypeStruct((rows * count, width), value.dtype)
    return value, out, [DMA((count,))] * 4, share_task(halo, part * width), True, False


def frames_gather(value):
    count = lax.axis_size("tm")
    out = jax.ShapeDtypeStruct((value.shape[0] * count, value.shape[1]), value.dtype)
    return value, out, [DMA((count,))] * 2, frames_gather_body, True, False


def frames_reduce(value):
    count = lax.axis_size("tm")
    landed = pltpu.VMEM((count, value.shape[0], value.shape[1] // count), value.dtype)
    return value, jax.ShapeDtypeStruct(value.shape, value.dtype), [landed] + [DMA((count,))] * 4, reduce_body, True, False


def together(number, *tasks):
    along_chan = any(not task[4] for task in tasks) or any(len(task[2]) == 4 for task in tasks)
    along_tm = any(task[4] for task in tasks)
    edges = any(task[5] for task in tasks)

    def kernel(*refs):
        tm, chan, core, chips, partner, at = chan_place()
        count = lax.axis_size("tm")
        greeted = []
        if along_chan:
            greeted += [partner] + [(tm, at(step)) for step in range(1, chips)]
        if along_tm:
            greeted += [((tm + step) % count, chan) for step in range(1, count)]
        elif edges:
            greeted += [((tm + 1) % count, chan), ((tm + count - 1) % count, chan)]
        greet(greeted)
        size = len(tasks)
        place = 2 * size
        bodies = []
        for index, task in enumerate(tasks):
            scratch = refs[place : place + len(task[2])]
            place += len(task[2])
            bodies.append(task[3](refs[index], refs[size + index], *scratch))
        for phase in range(3):
            for body in bodies:
                next(body, None)

    whole = pl.BlockSpec(memory_space=pltpu.VMEM)
    return pl.pallas_call(
        kernel,
        out_shape=[task[1] for task in tasks],
        in_specs=[whole] * len(tasks),
        out_specs=[whole] * len(tasks),
        scratch_shapes=[item for task in tasks for item in task[2]],
        compiler_params=pltpu.CompilerParams(
            collective_id=number, has_side_effects=True, vmem_limit_bytes=VMEM_LIMIT
        ),
    )(*[task[0] for task in tasks])


def saliency_kernel(spacings, pad, taps, ids_ref, eff_ref, *refs):
    units = len(spacings)
    grads, firsts = refs[:units], refs[units : 3 * units]
    o_ref, turned = refs[3 * units], refs[3 * units + 1]
    rows = turned.shape[1]
    width = ids_ref.shape[1]
    chunk = 512
    for unit in range(units):
        for tap in range(taps):
            shift = (tap - taps // 2) * spacings[unit]

            @pl.loop(0, rows // chunk)
            def _(block):
                start = pl.multiple_of(block * chunk, chunk)
                window = grads[unit][pl.ds(start + pad - shift, chunk)]
                same = ids_ref[pl.ds(start + pad - shift, chunk)] == ids_ref[pl.ds(start + pad, chunk)]
                kept = jnp.where(same, window, 0.0)
                turned[pl.ds(tap * width, width), pl.ds(start, chunk)] = kept.T.astype(turned.dtype)

        for half in range(2):
            source = firsts[2 * unit + half]
            span = source.shape[1]
            step = 256

            @pl.loop(0, span // step)
            def _(block):
                inner = pl.ds(pl.multiple_of(block * step, step), step)
                outer = pl.ds(pl.multiple_of(half * span + block * step, step), step)
                grad = jnp.dot(turned[...], source[:, inner], preferred_element_type=F32)
                o_ref[unit, :, outer] = eff_ref[unit, :, outer].astype(F32) * grad


def saliency(spacings, pad, taps, ids, eff, grads, firsts):
    whole = pl.BlockSpec(memory_space=pltpu.VMEM)
    operands = [ids, eff] + grads + firsts
    return pl.pallas_call(
        functools.partial(saliency_kernel, spacings, pad, taps),
        out_shape=jax.ShapeDtypeStruct(eff.shape, F32),
        in_specs=[whole] * len(operands),
        out_specs=whole,
        scratch_shapes=[pltpu.VMEM((eff.shape[1], firsts[0].shape[0]), BF16)],
        compiler_params=pltpu.CompilerParams(vmem_limit_bytes=VMEM_LIMIT),
    )(*operands)


def tm_scatter_kernel(x_ref, o_ref, landed, send, recv):
    tm, chan = lax.axis_index("tm"), lax.axis_index("chan")
    count = lax.axis_size("tm")
    rows = o_ref.shape[0]
    greet([((tm + step) % count, chan) for step in range(1, count)])
    started = []
    for step in range(1, count):
        to = (tm + step) % count
        copy = remote(
            x_ref.at[pl.ds(pl.multiple_of(to * rows, rows), rows)],
            landed.at[step],
            send.at[step],
            recv.at[step],
            (to, chan),
        )
        copy.start()
        started.append(copy)
    o_ref[...] = x_ref[pl.ds(pl.multiple_of(tm * rows, rows), rows)].astype(F32)
    for step in range(1, count):
        started[step - 1].wait_recv()
        o_ref[...] += landed[step].astype(F32)
    for copy in started:
        copy.wait_send()


def turn_kernel(x_ref, o_ref, send, recv):
    tm, chan = lax.axis_index("tm"), lax.axis_index("chan")
    frames, chans = lax.axis_size("tm"), lax.axis_size("chan")
    ratio = chans // frames
    rows, width = x_ref.shape
    target = chan // ratio
    own = target == tm
    barrier = pltpu.get_barrier_semaphore()
    for frame in range(frames):
        for part in range(ratio):
            source = (frame, tm * ratio + part)

            @pl.when(jnp.logical_or(frame != tm, source[1] != chan))
            def _():
                pl.semaphore_signal(barrier, inc=1, device_id=source, device_id_type=MESH)

    @pl.when(own)
    def _():
        pl.semaphore_wait(barrier, chans - 1)

    @pl.when(jnp.logical_not(own))
    def _():
        pl.semaphore_wait(barrier, chans)

    slot_rows = pl.ds(pl.multiple_of(tm * rows, rows), rows)
    slot_columns = column(chan % ratio, width)
    which = tm * ratio + chan % ratio

    def outgoing(step):
        return remote(
            x_ref,
            o_ref.at[slot_rows, slot_columns],
            send.at[step],
            recv.at[which],
            (target, (chan + step) % chans),
        )

    for step in range(1, chans):
        outgoing(step).start()

    @pl.when(own)
    def _():
        o_ref[slot_rows, slot_columns] = x_ref[...]

    @pl.when(jnp.logical_not(own))
    def _():
        outgoing(0).start()

    for frame in range(frames):
        for part in range(ratio):

            @pl.when(jnp.logical_or(frame != tm, tm * ratio + part != chan))
            def _():
                landing = o_ref.at[pl.ds(frame * rows, rows), pl.ds(part * width, width)]
                remote(
                    landing, landing, send.at[0], recv.at[frame * ratio + part], (tm, chan)
                ).wait_recv()

    for step in range(1, chans):
        outgoing(step).wait_send()

    @pl.when(jnp.logical_not(own))
    def _():
        outgoing(0).wait_send()


def run(kernel, out_shape, dtype, scratch, number, value):
    whole = pl.BlockSpec(memory_space=pltpu.VMEM)
    return pl.pallas_call(
        kernel,
        out_shape=jax.ShapeDtypeStruct(out_shape, dtype),
        in_specs=[whole],
        out_specs=whole,
        scratch_shapes=scratch,
        compiler_params=pltpu.CompilerParams(
            collective_id=number, has_side_effects=True, vmem_limit_bytes=VMEM_LIMIT
        ),
    )(value)


def plain_kernels(*widths):
    return all(width % 128 == 0 for width in widths)


def with_halo(cells, width):
    count = lax.axis_size("tm")
    head, tail = cells[:width], cells[-width:]
    return jnp.concatenate(
        [
            lax.ppermute(tail, "tm", [(i, (i + 1) % count) for i in range(count)]),
            cells,
            lax.ppermute(head, "tm", [((i + 1) % count, i) for i in range(count)]),
        ],
        axis=0,
    )


def tm_scatter(value, number):
    count = lax.axis_size("tm")
    rows, width = value.shape[0] // count, value.shape[1]
    if not plain_kernels(width):
        return lax.psum_scatter(value, "tm", scatter_dimension=0, tiled=True).astype(F32)
    dma = pltpu.SemaphoreType.DMA
    return run(
        tm_scatter_kernel,
        (rows, width),
        F32,
        [pltpu.VMEM((count, rows, width), value.dtype)] + [dma((count,))] * 2,
        number,
        value,
    )


def turn(value, number):
    frames, chans = lax.axis_size("tm"), lax.axis_size("chan")
    rows, width = value.shape
    if not plain_kernels(width) or chans % frames:
        return lax.all_to_all(
            lax.all_gather(value, "chan", axis=1, tiled=True), "tm", split_axis=1, concat_axis=0, tiled=True
        )
    return run(
        turn_kernel,
        (rows * frames, width * chans // frames),
        value.dtype,
        [pltpu.SemaphoreType.DMA((chans,))] * 2,
        number,
        value,
    )


def snake_act(values, alpha):
    return values + jnp.sin(alpha * values) ** 2 / alpha


def snake_slope(values, alpha):
    return 1.0 + jnp.sin(2.0 * alpha * values)


def track_ids(lengths, frame_index, total_frames):
    starts = jnp.cumsum(lengths) - lengths
    found = jnp.sum((starts[:, None] <= frame_index[None, :]).astype(jnp.int32), axis=0) - 1
    return jnp.where(frame_index < 0, -1, jnp.where(frame_index >= total_frames, -2, found))


def dot_last(left, right):
    return lax.dot_general(left, right, (((1,), (1,)), ((), ())), preferred_element_type=F32)


def dot_first(left, right):
    return lax.dot_general(left, right, (((0,), (0,)), ((), ())), preferred_element_type=F32)


def expand(kernel, mask):
    width, blocks = kernel.shape[-1], mask.shape[-1]
    spread = (
        jnp.arange(width, dtype=jnp.int32)[None, :] // (width // blocks)
        == jnp.arange(blocks, dtype=jnp.int32)[:, None]
    ).astype(BF16)
    keep = jnp.dot(mask.reshape(-1, blocks).astype(BF16), spread, preferred_element_type=F32)
    return (kernel.reshape(-1, width) * keep.astype(BF16)).reshape(kernel.shape)


def per_device(
    latent_input,
    upsample_kernel,
    dilated_kernel,
    pointwise_kernel,
    dilated_prune_mask,
    pointwise_prune_mask,
    snake_freq_upsample,
    snake_freq_dilated,
    snake_freq_pointwise,
    segment_lengths,
    cotangent,
):
    taps, out_local, in_local = upsample_kernel.shape
    stride = taps // 2
    half = stride // 2
    frame_count = latent_input.shape[1]
    rows = frame_count * stride
    tm_count = lax.axis_size("tm")
    tm_index = lax.axis_index("tm")
    total_frames = frame_count * tm_count
    units, kernel_taps, _, channels = dilated_kernel.shape

    def tap_mask(pos, offset):
        own = track_ids(segment_lengths, jnp.floor_divide(pos, stride), total_frames)
        other = track_ids(segment_lengths, jnp.floor_divide(pos + offset, stride), total_frames)
        return (own == other)[:, None]

    row_pos = tm_index * rows + jnp.arange(rows, dtype=jnp.int32)
    frame_pos = jnp.arange(total_frames, dtype=jnp.int32)

    dil_eff = expand(dilated_kernel, dilated_prune_mask)
    point_eff = expand(pointwise_kernel, pointwise_prune_mask)

    act = snake_act(latent_input.astype(F32), snake_freq_upsample[:, None]).astype(BF16).T
    cot = cotangent.T
    grad_second_last = lax.psum_scatter(
        jnp.dot(cot, point_eff[units - 1], preferred_element_type=F32).astype(BF16),
        "chan",
        scatter_dimension=1,
        tiled=True,
    ).astype(F32)

    act_all = turn(act, 0)
    product = dot_last(act_all, upsample_kernel.reshape(taps * out_local, in_local)).reshape(
        total_frames, taps, out_local
    )
    frame_ids = track_ids(segment_lengths, frame_pos, total_frames)
    prev_ok = (frame_ids == track_ids(segment_lengths, frame_pos - 1, total_frames))[:, None, None]
    next_ok = (frame_ids == track_ids(segment_lengths, frame_pos + 1, total_frames))[:, None, None]
    low = jnp.pad(product[:-1, half + stride :], ((1, 0), (0, 0), (0, 0)))
    high = jnp.pad(product[1:, :half], ((0, 1), (0, 0), (0, 0)))
    partial = product[:, half : half + stride] + jnp.concatenate(
        [jnp.where(prev_ok, low, 0.0), jnp.where(next_ok, high, 0.0)], axis=1
    )
    hidden = tm_scatter(partial.astype(BF16).reshape(rows * tm_count, out_local), 1)

    spacings = [3 ** (unit + 1) for unit in range(units)]
    reach = [(kernel_taps // 2) * spacing for spacing in spacings]
    flat = dil_eff.reshape(units, kernel_taps * out_local, channels)
    fast = units == 2 and plain_kernels(out_local, channels // 4, channels // tm_count) and frame_count % 16 == 0 and rows * tm_count % 512 == 0

    def conv_of(first_all, unit, halo):
        spans = dot_last(first_all, flat[unit])
        conv = jnp.zeros((rows, out_local), F32)
        for tap in range(kernel_taps):
            shift = (tap - kernel_taps // 2) * spacings[unit]
            piece = spans[halo + shift : halo + shift + rows, tap * out_local : (tap + 1) * out_local]
            conv = conv + jnp.where(tap_mask(row_pos, shift), piece, 0.0)
        return conv

    def first_of(hidden, unit):
        return snake_act(hidden, snake_freq_dilated[unit]).astype(BF16)

    def second_of(conv, unit):
        return snake_act(conv, snake_freq_pointwise[unit]).astype(BF16)

    def grad_conv_of(grad_second, conv, unit):
        return (grad_second * snake_slope(conv, snake_freq_pointwise[unit])).astype(BF16)

    def spread_back(grad_b, unit):
        return jnp.dot(grad_b, point_eff[unit], preferred_element_type=F32).astype(BF16)

    def shifted_taps(grad_wide, unit, halo):
        pieces = []
        for tap in range(kernel_taps):
            shift = (tap - kernel_taps // 2) * spacings[unit]
            window = grad_wide[halo - shift : halo - shift + rows]
            pieces.append(jnp.where(tap_mask(row_pos, -shift), window, jnp.zeros((), BF16)))
        return jnp.concatenate(pieces, axis=1)

    def outputs(decoded, dil, point_sums):
        return (
            decoded.astype(BF16).T,
            dil.reshape(units, kernel_taps, out_local, channels),
            point_eff.astype(F32) * point_sums.astype(F32),
        )

    if fast:
        halos = [-(-margin // 16) * 16 for margin in reach]
        (wide0,) = together(2, chan_gather(first_of(hidden, 0), halos[0]))
        conv0 = conv_of(wide0, 0, halos[0])
        second0, frames00 = together(3, chan_gather(second_of(conv0, 0), 0), share(wide0, halos[0], 0, 2))
        hidden1 = hidden + dot_last(second0, point_eff[0])
        wide1, frames01 = together(
            4, chan_gather(first_of(hidden1, 1), halos[1]), share(wide0, halos[0], 1, 2)
        )
        conv1 = conv_of(wide1, 1, halos[1])
        grad_conv1 = grad_conv_of(grad_second_last, conv1, 1)
        grads1, second1 = together(5, frames_gather(grad_conv1), chan_gather(second_of(conv1, 1), 0))
        decoded = hidden1 + dot_last(second1, point_eff[1])
        pad = halos[1]
        grads1 = jnp.pad(grads1, ((pad, pad), (0, 0)))
        window = lax.dynamic_slice_in_dim(grads1, tm_index * rows, rows + 2 * pad, axis=0)
        partial1 = jnp.dot(
            shifted_taps(window, 1, pad), flat[1], preferred_element_type=F32
        ).astype(BF16)
        grad_first, frames10 = together(6, chan_scatter(partial1), share(wide1, halos[1], 0, 2))
        grad_b0 = (cot.astype(F32) + grad_first * snake_slope(hidden1, snake_freq_dilated[1])).astype(BF16)
        point_parts = jnp.concatenate([dot_first(grad_b0, second0), dot_first(cot, second1)]).astype(BF16)
        grad_second0, frames11, point_sums = together(
            7, chan_scatter(spread_back(grad_b0, 0)), share(wide1, halos[1], 1, 2), frames_reduce(point_parts)
        )
        (grads0,) = together(8, frames_gather(grad_conv_of(grad_second0, conv0, 0)))
        grads0 = jnp.pad(grads0, ((pad, pad), (0, 0)))
        wide_pos = jnp.arange(rows * tm_count + 2 * pad, dtype=jnp.int32) - pad
        ids = track_ids(segment_lengths, jnp.floor_divide(wide_pos, stride), total_frames).astype(F32)
        dil = saliency(
            spacings,
            pad,
            kernel_taps,
            jnp.broadcast_to(ids[:, None], (ids.shape[0], out_local)),
            flat,
            [grads0.astype(F32), grads1.astype(F32)],
            [frames00, frames01, frames10, frames11],
        )
        return outputs(decoded, dil, point_sums.reshape(point_eff.shape))

    saved = []
    for unit in range(units):
        first = first_of(hidden, unit)
        wide = lax.all_gather(with_halo(first, reach[unit]), "chan", axis=1, tiled=True)
        conv = conv_of(wide, unit, reach[unit])
        second = lax.all_gather(second_of(conv, unit), "chan", axis=1, tiled=True)
        saved.append((hidden, wide[reach[unit] : reach[unit] + rows], conv, second))
        hidden = hidden + dot_last(second, point_eff[unit])
    grad_out = cot.astype(F32)
    parts = [None] * (2 * units)
    for unit in reversed(range(units)):
        hidden_in, first_own, conv, second = saved[unit]
        grad_b = grad_out.astype(BF16)
        if unit == units - 1:
            grad_second = grad_second_last
        else:
            grad_second = lax.psum_scatter(
                spread_back(grad_b, unit), "chan", scatter_dimension=1, tiled=True
            ).astype(F32)
        grad_conv = grad_conv_of(grad_second, conv, unit)
        shifted = shifted_taps(with_halo(grad_conv, reach[unit]), unit, reach[unit])
        parts[unit] = dot_first(shifted, first_own).astype(BF16)
        parts[units + unit] = dot_first(grad_b, second).astype(BF16)
        if unit > 0:
            back = jnp.dot(shifted, flat[unit], preferred_element_type=F32).astype(BF16)
            grad_first = lax.psum_scatter(back, "chan", scatter_dimension=1, tiled=True).astype(F32)
            grad_out = grad_out + grad_first * snake_slope(hidden_in, snake_freq_dilated[unit])
    sums = lax.psum(parts, "tm")
    dil = flat.astype(F32) * jnp.stack(sums[:units]).astype(F32)
    return outputs(hidden, dil, jnp.stack(sums[units:]))


def solution(mesh):
    return jax.shard_map(
        per_device,
        mesh=mesh,
        in_specs=(
            P("chan", "tm"),
            P(None, "chan", "tm"),
            P(None, None, "chan", None),
            P(None, "chan", None),
            P(None, None, "chan", None),
            P(None, "chan", None),
            P("chan"),
            P(None, "chan"),
            P(None, "chan"),
            P(),
            P("chan", "tm"),
        ),
        out_specs=(P("chan", "tm"), P(None, None, "chan", None), P(None, "chan", None)),
        check_vma=False,
    )
```

```python
import functools

import jax
import jax.numpy as jnp
from jax import lax
from jax.experimental import pallas as pl
from jax.experimental.pallas import tpu as pltpu
from jax.sharding import PartitionSpec as P

MESH = pl.DeviceIdType.MESH
BF16 = jnp.bfloat16
F32 = jnp.float32
VMEM_LIMIT = 48 * 1024 * 1024


def remote(src, dst, send, recv, device):
    return pltpu.make_async_remote_copy(
        src_ref=src, dst_ref=dst, send_sem=send, recv_sem=recv, device_id=device, device_id_type=MESH
    )


def greet(devices):
    barrier = pltpu.get_barrier_semaphore()
    for device in devices:
        pl.semaphore_signal(barrier, inc=1, device_id=device, device_id_type=MESH)
    pl.semaphore_wait(barrier, len(devices))


def chan_place():
    tm, chan = lax.axis_index("tm"), lax.axis_index("chan")
    chips = lax.axis_size("chan") // 2
    chip, core = chan // 2, chan % 2
    partner = (tm, chan + 1 - 2 * core)

    def at(step):
        return ((chip + step + chips) % chips) * 2 + core

    return tm, chan, core, chips, partner, at


def column(index, width):
    return pl.ds(pl.multiple_of(index * width, width), width)


def chan_gather_task(halo):
    def body(x_ref, o_ref, send, recv, fsend, frecv):
        tm, chan, core, chips, partner, at = chan_place()
        frames = lax.axis_size("tm")
        rows, width = x_ref.shape
        mine = column(chan, width)
        other = 1 - 2 * core
        parts = [(pl.ds(halo, rows), x_ref, tm, range(1, chips))]
        if halo:
            parts += [
                (pl.ds(0, halo), x_ref.at[pl.ds(rows - halo, halo)], (tm + 1) % frames, range(chips)),
                (pl.ds(halo + rows, halo), x_ref.at[pl.ds(0, halo)], (tm + frames - 1) % frames, range(chips)),
            ]
        started = []

        def begin(copy):
            copy.start()
            started.append(copy)

        for part, (span, source, to, steps) in enumerate(parts):
            for step in steps:
                begin(remote(source, o_ref.at[span, mine], send.at[part, step], recv.at[part, step], (to, at(step))))
        begin(remote(x_ref, o_ref.at[parts[0][0], mine], fsend.at[0, 0], frecv.at[0, 0], partner))
        yield
        o_ref[parts[0][0], mine] = x_ref[...]
        for step in range(chips):
            for part, (span, source, to, steps) in enumerate(parts):
                if step in steps:
                    slot = o_ref.at[span, column(at(-step), width)]
                    remote(slot, slot, send.at[part, step], recv.at[part, step], partner).wait_recv()
                    begin(remote(slot, slot, fsend.at[part, step], frecv.at[part, step], partner))
        yield
        for part, (span, source, to, steps) in enumerate(parts):
            for step in range(chips):
                slot = o_ref.at[span, column(at(-step) + other, width)]
                remote(slot, slot, fsend.at[part, step], frecv.at[part, step], partner).wait_recv()
        for copy in started:
            copy.wait_send()

    return body


def chan_scatter_body(x_ref, o_ref, pair, summed, landed, psend, precv, send, recv):
    tm, chan, core, chips, partner, at = chan_place()
    width = o_ref.shape[1]
    other = 1 - 2 * core
    order = list(range(1, chips)) + [0]
    started = []
    pairs = {}
    for step in order:
        copy = remote(
            x_ref.at[:, column(at(step) + other, width)], pair.at[step], psend.at[step], precv.at[step], partner
        )
        copy.start()
        pairs[step] = copy
    yield
    for step in range(1, chips):
        pairs[step].wait_recv()
        summed[step] = (
            x_ref[:, column(at(step), width)].astype(F32) + pair[step].astype(F32)
        ).astype(summed.dtype)
        copy = remote(summed.at[step], landed.at[step], send.at[step], recv.at[step], (tm, at(step)))
        copy.start()
        started.append(copy)
    pairs[0].wait_recv()
    o_ref[...] = x_ref[:, column(chan, width)].astype(F32) + pair[0].astype(F32)
    yield
    for copy, step in zip(started, range(1, chips)):
        copy.wait_recv()
        o_ref[...] += landed[step].astype(F32)
    for copy in started:
        copy.wait_send()
    for step in order:
        pairs[step].wait_send()


def share_task(halo, base):
    def body(x_ref, o_ref, send, recv, fsend, frecv):
        tm, chan, core, chips, partner, at = chan_place()
        count = lax.axis_size("tm")
        rows, width = o_ref.shape[0] // count, o_ref.shape[1] // 2
        own = pl.ds(halo, rows)

        def slot(index, half):
            return o_ref.at[pl.ds(pl.multiple_of(index * rows, rows), rows), column(half, width)]

        started = []
        source = x_ref.at[own, pl.ds(pl.multiple_of(base + core * width, width), width)]
        for step in range(1, count):
            copy = remote(source, slot(tm, core), send.at[step], recv.at[step], ((tm + step) % count, chan))
            copy.start()
            started.append(copy)
        yield
        o_ref[pl.ds(pl.multiple_of(tm * rows, rows), rows), :] = x_ref[own, pl.ds(base, 2 * width)]
        for step in range(1, count):
            landing = slot((tm + count - step) % count, core)
            remote(landing, landing, send.at[step], recv.at[step], partner).wait_recv()
            copy = remote(landing, landing, fsend.at[step], frecv.at[step], partner)
            copy.start()
            started.append(copy)
        yield
        for step in range(1, count):
            landing = slot((tm + count - step) % count, 1 - core)
            remote(landing, landing, send.at[step], frecv.at[step], partner).wait_recv()
        for copy in started:
            copy.wait_send()

    return body


def frames_gather_body(x_ref, o_ref, send, recv):
    tm, chan = lax.axis_index("tm"), lax.axis_index("chan")
    count = lax.axis_size("tm")
    rows = x_ref.shape[0]

    def slot(index):
        return o_ref.at[pl.ds(pl.multiple_of(index * rows, rows), rows)]

    started = []
    for step in range(1, count):
        copy = remote(x_ref, slot(tm), send.at[step], recv.at[step], ((tm + step) % count, chan))
        copy.start()
        started.append(copy)
    yield
    o_ref[pl.ds(pl.multiple_of(tm * rows, rows), rows)] = x_ref[...]
    yield
    for step in range(1, count):
        landing = slot((tm + count - step) % count)
        remote(landing, landing, send.at[step], recv.at[step], (tm, chan)).wait_recv()
    for copy in started:
        copy.wait_send()


def reduce_body(x_ref, o_ref, landed, send, recv, gsend, grecv):
    tm, chan = lax.axis_index("tm"), lax.axis_index("chan")
    count = lax.axis_size("tm")
    width = x_ref.shape[1] // count
    started = []
    for step in range(1, count):
        to = (tm + step) % count
        copy = remote(x_ref.at[:, column(to, width)], landed.at[step], send.at[step], recv.at[step], (to, chan))
        copy.start()
        started.append(copy)
    yield
    total = x_ref[:, column(tm, width)].astype(F32)
    for step in range(1, count):
        started[step - 1].wait_recv()
        total += landed[step].astype(F32)
    mine = o_ref.at[:, column(tm, width)]
    o_ref[:, column(tm, width)] = total.astype(o_ref.dtype)
    for step in range(1, count):
        copy = remote(mine, mine, gsend.at[step], grecv.at[step], ((tm + step) % count, chan))
        copy.start()
        started.append(copy)
    yield
    for step in range(1, count):
        landing = o_ref.at[:, column((tm + count - step) % count, width)]
        remote(landing, landing, send.at[step], grecv.at[step], (tm, chan)).wait_recv()
    for copy in started:
        copy.wait_send()


DMA = pltpu.SemaphoreType.DMA


def chan_gather(value, halo):
    rows, width = value.shape
    chans = lax.axis_size("chan")
    out = jax.ShapeDtypeStruct((rows + 2 * halo, width * chans), value.dtype)
    return (value,), out, [DMA((3, chans // 2))] * 4, chan_gather_task(halo), ("chan", "edge") if halo else ("chan",)


def chan_scatter(value):
    rows, chans = value.shape[0], lax.axis_size("chan")
    width, chips = value.shape[1] // chans, chans // 2
    scratch = [pltpu.VMEM((chips, rows, width), value.dtype)] * 3 + [DMA((chips,))] * 4
    return (value,), jax.ShapeDtypeStruct((rows, width), F32), scratch, chan_scatter_body, ("chan",)


def share(value, halo, part, parts):
    count = lax.axis_size("tm")
    rows, width = value.shape[0] - 2 * halo, value.shape[1] // parts
    out = jax.ShapeDtypeStruct((rows * count, width), value.dtype)
    return (value,), out, [DMA((count,))] * 4, share_task(halo, part * width), ("chan", "tm")


def frames_gather(value):
    count = lax.axis_size("tm")
    out = jax.ShapeDtypeStruct((value.shape[0] * count, value.shape[1]), value.dtype)
    return (value,), out, [DMA((count,))] * 2, frames_gather_body, ("tm",)


def frames_reduce(value):
    count = lax.axis_size("tm")
    landed = pltpu.VMEM((count, value.shape[0], value.shape[1] // count), value.dtype)
    scratch = [landed] + [DMA((count,))] * 4
    return (value,), jax.ShapeDtypeStruct(value.shape, value.dtype), scratch, reduce_body, ("tm",)


def frames_scatter(value):
    count = lax.axis_size("tm")
    rows, width = value.shape[0] // count, value.shape[1]
    scratch = [pltpu.VMEM((count, rows, width), value.dtype)] + [DMA((count,))] * 2
    return (value,), jax.ShapeDtypeStruct((rows, width), F32), scratch, frames_scatter_body, ("tm",)


def expand_body(kernel_ref, mask_ref, o_ref):
    yield
    rows, width = kernel_ref.shape
    blocks = mask_ref.shape[1]
    spread = (
        lax.broadcasted_iota(jnp.int32, (blocks, width), 1) // (width // blocks)
        == lax.broadcasted_iota(jnp.int32, (blocks, width), 0)
    ).astype(F32).astype(BF16)
    step = 256

    @pl.loop(0, rows // step)
    def _(block):
        span = pl.ds(pl.multiple_of(block * step, step), step)
        keep = jnp.dot(mask_ref[span].astype(F32).astype(BF16), spread, preferred_element_type=F32)
        o_ref[span] = (kernel_ref[span].astype(F32) * keep).astype(o_ref.dtype)

    yield


def expand_task(kernel, mask):
    return (kernel, mask), jax.ShapeDtypeStruct(kernel.shape, kernel.dtype), [], expand_body, ()


def together(number, *tasks):
    axes = set(axis for task in tasks for axis in task[4])
    inputs = [item for task in tasks for item in task[0]]

    def kernel(*refs):
        tm, chan, core, chips, partner, at = chan_place()
        count = lax.axis_size("tm")
        greeted = []
        if "chan" in axes:
            greeted += [partner] + [(tm, at(step)) for step in range(1, chips)]
        if "tm" in axes:
            greeted += [((tm + step) % count, chan) for step in range(1, count)]
        elif "edge" in axes:
            greeted += [((tm + 1) % count, chan), ((tm + count - 1) % count, chan)]
        if "edge" in axes:
            for step in range(1, chips):
                greeted += [((tm + 1) % count, at(step)), ((tm + count - 1) % count, at(step))]
        greet(greeted)
        taken, out, place = 0, len(inputs), len(inputs) + len(tasks)
        bodies = []
        for task in tasks:
            used = refs[taken : taken + len(task[0])] + (refs[out],) + refs[place : place + len(task[2])]
            taken, out, place = taken + len(task[0]), out + 1, place + len(task[2])
            bodies.append(task[3](*used))
        for phase in range(3):
            for body in bodies:
                next(body, None)

    whole = pl.BlockSpec(memory_space=pltpu.VMEM)
    return pl.pallas_call(
        kernel,
        out_shape=[task[1] for task in tasks],
        in_specs=[whole] * len(inputs),
        out_specs=[whole] * len(tasks),
        scratch_shapes=[item for task in tasks for item in task[2]],
        compiler_params=pltpu.CompilerParams(
            collective_id=number, has_side_effects=True, vmem_limit_bytes=VMEM_LIMIT
        ),
    )(*inputs)


def taps_kernel(halo, spacing, taps, x_ref, w_ref, ids_ref, alpha_ref, conv_ref, second_ref, spans):
    rows, width = conv_ref.shape
    step = 2 * width
    total = taps * width
    for base in range(0, total, step):
        span = pl.ds(base, min(step, total - base))
        spans[:, span] = lax.dot_general(
            x_ref[...], w_ref[span], (((1,), (1,)), ((), ())), preferred_element_type=F32
        )
    alpha = alpha_ref[...]
    chunk = 128 if rows % 128 == 0 else rows
    for start in range(0, rows, chunk):
        own = ids_ref[pl.ds(start + halo, chunk)]
        conv = jnp.zeros((chunk, width), F32)
        for tap in range(taps):
            window = pl.ds(start + halo + (tap - taps // 2) * spacing, chunk)
            conv = conv + jnp.where(ids_ref[window] == own, spans[window, pl.ds(tap * width, width)], 0.0)
        conv_ref[pl.ds(start, chunk)] = conv
        second_ref[pl.ds(start, chunk)] = snake_act(conv, alpha).astype(second_ref.dtype)


def taps_call(wide, weights, ids, alpha, halo, spacing, taps):
    rows, width = wide.shape[0] - 2 * halo, weights.shape[0] // taps
    whole = pl.BlockSpec(memory_space=pltpu.VMEM)
    return pl.pallas_call(
        functools.partial(taps_kernel, halo, spacing, taps),
        out_shape=[jax.ShapeDtypeStruct((rows, width), F32), jax.ShapeDtypeStruct((rows, width), BF16)],
        in_specs=[whole] * 4,
        out_specs=[whole] * 2,
        scratch_shapes=[pltpu.VMEM((wide.shape[0], weights.shape[0]), F32)],
        compiler_params=pltpu.CompilerParams(vmem_limit_bytes=VMEM_LIMIT),
    )(wide, weights, ids, alpha)


def saliency_kernel(spacings, taps, mask_ref, *refs):
    units = len(spacings)
    grads, eff_ref, firsts = refs[:units], refs[units], refs[units + 1 : 3 * units + 1]
    o_ref, flipped, turned, eff, first, made, loads, stores = refs[3 * units + 1 :]
    rows, width = grads[0].shape
    order = list(reversed(range(units)))
    span = firsts[0].shape[1]
    copies = {}
    for unit in order:
        copies[unit] = [
            pltpu.make_async_copy(
                firsts[2 * unit + half], first.at[unit, :, pl.ds(half * span, span)], loads.at[unit, half]
            )
            for half in range(2)
        ] + [pltpu.make_async_copy(eff_ref.at[unit], eff.at[unit], loads.at[unit, 2])]
        for copy in copies[unit]:
            copy.start()
    chunk, lines, step = 512, 16, 256
    blocks = 2 * span // step
    for place, unit in enumerate(order):

        @pl.loop(0, rows // chunk)
        def _(block):
            part = pl.ds(pl.multiple_of(block * chunk, chunk), chunk)
            flipped[:, part] = grads[unit][part].astype(F32).T

        @pl.loop(0, width // lines)
        def _(block):
            values = flipped[pl.ds(pl.multiple_of(block * lines, lines), lines)]
            for tap in range(taps):
                shift = ((tap - taps // 2) * spacings[unit]) % rows
                moved = pltpu.roll(values, shift, 1) if shift else values
                kept = moved * mask_ref[pl.ds(unit * taps + tap, 1)]
                line = pl.multiple_of(tap * width + block * lines, lines)
                turned[pl.ds(line, lines)] = kept.astype(turned.dtype)

        for copy in copies[unit]:
            copy.wait()

        def store(slot, block):
            outer = pl.ds(pl.multiple_of(block * step, step), step)
            return pltpu.make_async_copy(made.at[slot], o_ref.at[unit, :, outer], stores.at[slot])

        @pl.loop(0, blocks)
        def _(block):
            slot = block % 2
            outer = pl.ds(pl.multiple_of(block * step, step), step)
            grad = jnp.dot(turned[...], first[unit, :, outer], preferred_element_type=F32)
            if place:
                store(slot, block).wait()
            else:

                @pl.when(block >= 2)
                def _():
                    store(slot, block).wait()

            made[slot] = eff[unit, :, outer].astype(F32) * grad
            store(slot, block).start()

        if place == units - 1:
            for slot in range(2):
                store(slot, slot).wait()


def saliency(spacings, taps, masks, eff, grads, firsts):
    whole, anywhere = pl.BlockSpec(memory_space=pltpu.VMEM), pl.BlockSpec(memory_space=pl.ANY)
    units = len(spacings)
    rows, width = grads[0].shape
    operands = [masks] + grads + [eff] + firsts
    return pl.pallas_call(
        functools.partial(saliency_kernel, spacings, taps),
        out_shape=jax.ShapeDtypeStruct(eff.shape, F32),
        in_specs=[whole] * (1 + units) + [anywhere] * (1 + 2 * units),
        out_specs=anywhere,
        scratch_shapes=[
            pltpu.VMEM((width, rows), F32),
            pltpu.VMEM((taps * width, rows), BF16),
            pltpu.VMEM(eff.shape, BF16),
            pltpu.VMEM((units, rows, eff.shape[2]), BF16),
            pltpu.VMEM((2, eff.shape[1], 256), F32),
            DMA((units, 3)),
            DMA((2,)),
        ],
        compiler_params=pltpu.CompilerParams(vmem_limit_bytes=VMEM_LIMIT),
    )(*operands)


def frames_scatter_body(x_ref, o_ref, landed, send, recv):
    tm, chan = lax.axis_index("tm"), lax.axis_index("chan")
    count = lax.axis_size("tm")
    rows = o_ref.shape[0]
    started = []
    for step in range(1, count):
        to = (tm + step) % count
        copy = remote(
            x_ref.at[pl.ds(pl.multiple_of(to * rows, rows), rows)],
            landed.at[step],
            send.at[step],
            recv.at[step],
            (to, chan),
        )
        copy.start()
        started.append(copy)
    yield
    o_ref[...] = x_ref[pl.ds(pl.multiple_of(tm * rows, rows), rows)].astype(F32)
    yield
    for step in range(1, count):
        started[step - 1].wait_recv()
        o_ref[...] += landed[step].astype(F32)
    for copy in started:
        copy.wait_send()


def turn_kernel(x_ref, o_ref, send, recv):
    tm, chan = lax.axis_index("tm"), lax.axis_index("chan")
    frames, chans = lax.axis_size("tm"), lax.axis_size("chan")
    ratio = chans // frames
    rows, width = x_ref.shape
    target = chan // ratio
    own = target == tm
    barrier = pltpu.get_barrier_semaphore()
    for frame in range(frames):
        for part in range(ratio):
            source = (frame, tm * ratio + part)

            @pl.when(jnp.logical_or(frame != tm, source[1] != chan))
            def _():
                pl.semaphore_signal(barrier, inc=1, device_id=source, device_id_type=MESH)

    @pl.when(own)
    def _():
        pl.semaphore_wait(barrier, chans - 1)

    @pl.when(jnp.logical_not(own))
    def _():
        pl.semaphore_wait(barrier, chans)

    slot_rows = pl.ds(pl.multiple_of(tm * rows, rows), rows)
    slot_columns = column(chan % ratio, width)
    which = tm * ratio + chan % ratio

    def outgoing(step):
        return remote(
            x_ref,
            o_ref.at[slot_rows, slot_columns],
            send.at[step],
            recv.at[which],
            (target, (chan + step) % chans),
        )

    for step in range(1, chans):
        outgoing(step).start()

    @pl.when(own)
    def _():
        o_ref[slot_rows, slot_columns] = x_ref[...]

    @pl.when(jnp.logical_not(own))
    def _():
        outgoing(0).start()

    for frame in range(frames):
        for part in range(ratio):

            @pl.when(jnp.logical_or(frame != tm, tm * ratio + part != chan))
            def _():
                landing = o_ref.at[pl.ds(frame * rows, rows), pl.ds(part * width, width)]
                remote(
                    landing, landing, send.at[0], recv.at[frame * ratio + part], (tm, chan)
                ).wait_recv()

    for step in range(1, chans):
        outgoing(step).wait_send()

    @pl.when(jnp.logical_not(own))
    def _():
        outgoing(0).wait_send()


def run(kernel, out_shape, dtype, scratch, number, value):
    whole = pl.BlockSpec(memory_space=pltpu.VMEM)
    return pl.pallas_call(
        kernel,
        out_shape=jax.ShapeDtypeStruct(out_shape, dtype),
        in_specs=[whole],
        out_specs=whole,
        scratch_shapes=scratch,
        compiler_params=pltpu.CompilerParams(
            collective_id=number, has_side_effects=True, vmem_limit_bytes=VMEM_LIMIT
        ),
    )(value)


def plain_kernels(*widths):
    return all(width % 128 == 0 for width in widths)


def with_halo(cells, width):
    count = lax.axis_size("tm")
    head, tail = cells[:width], cells[-width:]
    return jnp.concatenate(
        [
            lax.ppermute(tail, "tm", [(i, (i + 1) % count) for i in range(count)]),
            cells,
            lax.ppermute(head, "tm", [((i + 1) % count, i) for i in range(count)]),
        ],
        axis=0,
    )


def turn(value, number):
    frames, chans = lax.axis_size("tm"), lax.axis_size("chan")
    rows, width = value.shape
    if not plain_kernels(width) or chans % frames:
        return lax.all_to_all(
            lax.all_gather(value, "chan", axis=1, tiled=True), "tm", split_axis=1, concat_axis=0, tiled=True
        )
    return run(
        turn_kernel,
        (rows * frames, width * chans // frames),
        value.dtype,
        [pltpu.SemaphoreType.DMA((chans,))] * 2,
        number,
        value,
    )


def snake_act(values, alpha):
    return values + jnp.sin(alpha * values) ** 2 / alpha


def snake_slope(values, alpha):
    return 1.0 + jnp.sin(2.0 * alpha * values)


def track_ids(lengths, frame_index, total_frames):
    starts = jnp.cumsum(lengths) - lengths
    found = jnp.sum((starts[:, None] <= frame_index[None, :]).astype(jnp.int32), axis=0) - 1
    return jnp.where(frame_index < 0, -1, jnp.where(frame_index >= total_frames, -2, found))


def dot_last(left, right):
    return lax.dot_general(left, right, (((1,), (1,)), ((), ())), preferred_element_type=F32)


def dot_first(left, right):
    return lax.dot_general(left, right, (((0,), (0,)), ((), ())), preferred_element_type=F32)


def expand(kernel, mask):
    width, blocks = kernel.shape[-1], mask.shape[-1]
    spread = (
        jnp.arange(width, dtype=jnp.int32)[None, :] // (width // blocks)
        == jnp.arange(blocks, dtype=jnp.int32)[:, None]
    ).astype(BF16)
    keep = jnp.dot(mask.reshape(-1, blocks).astype(BF16), spread, preferred_element_type=F32)
    return (kernel.reshape(-1, width) * keep.astype(BF16)).reshape(kernel.shape)


def per_device(
    latent_input,
    upsample_kernel,
    dilated_kernel,
    pointwise_kernel,
    dilated_prune_mask,
    pointwise_prune_mask,
    snake_freq_upsample,
    snake_freq_dilated,
    snake_freq_pointwise,
    segment_lengths,
    cotangent,
):
    taps, out_local, in_local = upsample_kernel.shape
    stride = taps // 2
    half = stride // 2
    frame_count = latent_input.shape[1]
    rows = frame_count * stride
    tm_count = lax.axis_size("tm")
    tm_index = lax.axis_index("tm")
    total_frames = frame_count * tm_count
    units, kernel_taps, _, channels = dilated_kernel.shape

    def tap_mask(pos, offset):
        own = track_ids(segment_lengths, jnp.floor_divide(pos, stride), total_frames)
        other = track_ids(segment_lengths, jnp.floor_divide(pos + offset, stride), total_frames)
        return (own == other)[:, None]

    row_pos = tm_index * rows + jnp.arange(rows, dtype=jnp.int32)
    frame_pos = jnp.arange(total_frames, dtype=jnp.int32)

    point_eff = expand(pointwise_kernel, pointwise_prune_mask)

    act = snake_act(latent_input.astype(F32), snake_freq_upsample[:, None]).astype(BF16).T
    cot = cotangent.T
    grad_second_last = lax.psum_scatter(
        jnp.dot(cot, point_eff[units - 1], preferred_element_type=F32).astype(BF16),
        "chan",
        scatter_dimension=1,
        tiled=True,
    ).astype(F32)

    act_all = turn(act, 0)
    product = dot_last(act_all, upsample_kernel.reshape(taps * out_local, in_local)).reshape(
        total_frames, taps, out_local
    )
    frame_ids = track_ids(segment_lengths, frame_pos, total_frames)
    prev_ok = (frame_ids == track_ids(segment_lengths, frame_pos - 1, total_frames))[:, None, None]
    next_ok = (frame_ids == track_ids(segment_lengths, frame_pos + 1, total_frames))[:, None, None]
    low = jnp.pad(product[:-1, half + stride :], ((1, 0), (0, 0), (0, 0)))
    high = jnp.pad(product[1:, :half], ((0, 1), (0, 0), (0, 0)))
    partial = product[:, half : half + stride] + jnp.concatenate(
        [jnp.where(prev_ok, low, 0.0), jnp.where(next_ok, high, 0.0)], axis=1
    )
    partial = partial.astype(BF16).reshape(rows * tm_count, out_local)

    spacings = [3 ** (unit + 1) for unit in range(units)]
    reach = [(kernel_taps // 2) * spacing for spacing in spacings]
    fast = units == 2 and plain_kernels(out_local, channels // 4, channels // tm_count)
    fast = fast and frame_count % 16 == 0 and rows * tm_count % 512 == 0 and units * kernel_taps * out_local % 256 == 0

    def conv_of(first_all, unit, halo):
        spans = dot_last(first_all, flat[unit])
        conv = jnp.zeros((rows, out_local), F32)
        for tap in range(kernel_taps):
            shift = (tap - kernel_taps // 2) * spacings[unit]
            piece = spans[halo + shift : halo + shift + rows, tap * out_local : (tap + 1) * out_local]
            conv = conv + jnp.where(tap_mask(row_pos, shift), piece, 0.0)
        return conv

    def first_of(hidden, unit):
        return snake_act(hidden, snake_freq_dilated[unit]).astype(BF16)

    def second_of(conv, unit):
        return snake_act(conv, snake_freq_pointwise[unit]).astype(BF16)

    def grad_conv_of(grad_second, conv, unit):
        return (grad_second * snake_slope(conv, snake_freq_pointwise[unit])).astype(BF16)

    def spread_back(grad_b, unit):
        return jnp.dot(grad_b, point_eff[unit], preferred_element_type=F32).astype(BF16)

    def shifted_taps(grad_wide, unit, halo):
        pieces = []
        for tap in range(kernel_taps):
            shift = (tap - kernel_taps // 2) * spacings[unit]
            window = grad_wide[halo - shift : halo - shift + rows]
            pieces.append(jnp.where(tap_mask(row_pos, -shift), window, jnp.zeros((), BF16)))
        return jnp.concatenate(pieces, axis=1)

    def outputs(decoded, dil, point_sums):
        return (
            decoded.astype(BF16).T,
            dil.reshape(units, kernel_taps, out_local, channels),
            point_eff.astype(F32) * point_sums.astype(F32),
        )

    if fast:
        halos = [-(-margin // 16) * 16 for margin in reach]
        hidden, flat = together(
            1,
            frames_scatter(partial),
            expand_task(
                dilated_kernel.reshape(-1, channels),
                dilated_prune_mask.reshape(-1, dilated_prune_mask.shape[-1]),
            ),
        )
        flat = flat.reshape(units, kernel_taps * out_local, channels)

        def taps_of(wide, unit):
            pos = tm_index * rows - halos[unit] + jnp.arange(wide.shape[0], dtype=jnp.int32)
            ids = track_ids(segment_lengths, jnp.floor_divide(pos, stride), total_frames).astype(F32)
            ids = jnp.broadcast_to(ids[:, None], (wide.shape[0], out_local))
            alpha = snake_freq_pointwise[unit][None]
            return taps_call(wide, flat[unit], ids, alpha, halos[unit], spacings[unit], kernel_taps)

        (wide0,) = together(2, chan_gather(first_of(hidden, 0), halos[0]))
        conv0, mid0 = taps_of(wide0, 0)
        second0, frames00 = together(3, chan_gather(mid0, 0), share(wide0, halos[0], 0, 2))
        hidden1 = hidden + dot_last(second0, point_eff[0])
        wide1, frames01 = together(
            4, chan_gather(first_of(hidden1, 1), halos[1]), share(wide0, halos[0], 1, 2)
        )
        conv1, mid1 = taps_of(wide1, 1)
        grad_conv1 = grad_conv_of(grad_second_last, conv1, 1)
        grads1, second1 = together(5, frames_gather(grad_conv1), chan_gather(mid1, 0))
        decoded = hidden1 + dot_last(second1, point_eff[1])
        pad = halos[1]
        window = lax.dynamic_slice_in_dim(jnp.pad(grads1, ((pad, pad), (0, 0))), tm_index * rows, rows + 2 * pad, axis=0)
        partial1 = jnp.dot(
            shifted_taps(window, 1, pad), flat[1], preferred_element_type=F32
        ).astype(BF16)
        grad_first, points1, frames10 = together(
            6,
            chan_scatter(partial1),
            frames_reduce(dot_first(cot, second1).astype(BF16)),
            share(wide1, halos[1], 0, 2),
        )
        grad_b0 = (cot.astype(F32) + grad_first * snake_slope(hidden1, snake_freq_dilated[1])).astype(BF16)
        grad_second0, points0, frames11 = together(
            7,
            chan_scatter(spread_back(grad_b0, 0)),
            frames_reduce(dot_first(grad_b0, second0).astype(BF16)),
            share(wide1, halos[1], 1, 2),
        )
        (grads0,) = together(8, frames_gather(grad_conv_of(grad_second0, conv0, 0)))
        all_pos = jnp.arange(rows * tm_count, dtype=jnp.int32)
        masks = jnp.stack(
            [
                tap_mask(all_pos, -(tap - kernel_taps // 2) * spacing)[:, 0].astype(F32)
                for spacing in spacings
                for tap in range(kernel_taps)
            ]
        )
        dil = saliency(
            spacings, kernel_taps, masks, flat, [grads0, grads1], [frames00, frames01, frames10, frames11]
        )
        return outputs(decoded, dil, jnp.stack([points0, points1]))

    hidden = lax.psum_scatter(partial, "tm", scatter_dimension=0, tiled=True).astype(F32)
    flat = expand(dilated_kernel, dilated_prune_mask).reshape(units, kernel_taps * out_local, channels)
    saved = []
    for unit in range(units):
        first = first_of(hidden, unit)
        wide = lax.all_gather(with_halo(first, reach[unit]), "chan", axis=1, tiled=True)
        conv = conv_of(wide, unit, reach[unit])
        second = lax.all_gather(second_of(conv, unit), "chan", axis=1, tiled=True)
        saved.append((hidden, wide[reach[unit] : reach[unit] + rows], conv, second))
        hidden = hidden + dot_last(second, point_eff[unit])
    grad_out = cot.astype(F32)
    parts = [None] * (2 * units)
    for unit in reversed(range(units)):
        hidden_in, first_own, conv, second = saved[unit]
        grad_b = grad_out.astype(BF16)
        if unit == units - 1:
            grad_second = grad_second_last
        else:
            grad_second = lax.psum_scatter(
                spread_back(grad_b, unit), "chan", scatter_dimension=1, tiled=True
            ).astype(F32)
        grad_conv = grad_conv_of(grad_second, conv, unit)
        shifted = shifted_taps(with_halo(grad_conv, reach[unit]), unit, reach[unit])
        parts[unit] = dot_first(shifted, first_own).astype(BF16)
        parts[units + unit] = dot_first(grad_b, second).astype(BF16)
        if unit > 0:
            back = jnp.dot(shifted, flat[unit], preferred_element_type=F32).astype(BF16)
            grad_first = lax.psum_scatter(back, "chan", scatter_dimension=1, tiled=True).astype(F32)
            grad_out = grad_out + grad_first * snake_slope(hidden_in, snake_freq_dilated[unit])
    sums = lax.psum(parts, "tm")
    dil = flat.astype(F32) * jnp.stack(sums[:units]).astype(F32)
    return outputs(hidden, dil, jnp.stack(sums[units:]))


def solution(mesh):
    return jax.shard_map(
        per_device,
        mesh=mesh,
        in_specs=(
            P("chan", "tm"),
            P(None, "chan", "tm"),
            P(None, None, "chan", None),
            P(None, "chan", None),
            P(None, None, "chan", None),
            P(None, "chan", None),
            P("chan"),
            P(None, "chan"),
            P(None, "chan"),
            P(),
            P("chan", "tm"),
        ),
        out_specs=(P("chan", "tm"), P(None, None, "chan", None), P(None, "chan", None)),
        check_vma=False,
    )
```

```python
import functools

import jax
import jax.numpy as jnp
from jax import lax
from jax.experimental import pallas as pl
from jax.experimental.pallas import tpu as pltpu
from jax.sharding import PartitionSpec as P

MESH = pl.DeviceIdType.MESH
BF16 = jnp.bfloat16
F32 = jnp.float32
VMEM_LIMIT = 48 * 1024 * 1024


def remote(src, dst, send, recv, device):
    return pltpu.make_async_remote_copy(
        src_ref=src, dst_ref=dst, send_sem=send, recv_sem=recv, device_id=device, device_id_type=MESH
    )


def greet(devices):
    barrier = pltpu.get_barrier_semaphore()
    for device in devices:
        pl.semaphore_signal(barrier, inc=1, device_id=device, device_id_type=MESH)
    pl.semaphore_wait(barrier, len(devices))


def chan_place():
    tm, chan = lax.axis_index("tm"), lax.axis_index("chan")
    chips = lax.axis_size("chan") // 2
    chip, core = chan // 2, chan % 2
    partner = (tm, chan + 1 - 2 * core)

    def at(step):
        return ((chip + step + chips) % chips) * 2 + core

    return tm, chan, core, chips, partner, at


def column(index, width):
    return pl.ds(pl.multiple_of(index * width, width), width)


def chan_gather_task(halo):
    def body(x_ref, o_ref, send, recv, fsend, frecv):
        tm, chan, core, chips, partner, at = chan_place()
        frames = lax.axis_size("tm")
        rows, width = x_ref.shape
        mine = column(chan, width)
        other = 1 - 2 * core
        parts = [(pl.ds(halo, rows), x_ref, tm, range(1, chips))]
        if halo:
            parts += [
                (pl.ds(0, halo), x_ref.at[pl.ds(rows - halo, halo)], (tm + 1) % frames, range(chips)),
                (pl.ds(halo + rows, halo), x_ref.at[pl.ds(0, halo)], (tm + frames - 1) % frames, range(chips)),
            ]
        started = []

        def begin(copy):
            copy.start()
            started.append(copy)

        for part, (span, source, to, steps) in reversed(list(enumerate(parts))):
            for step in steps:
                begin(remote(source, o_ref.at[span, mine], send.at[part, step], recv.at[part, step], (to, at(step))))
        begin(remote(x_ref, o_ref.at[parts[0][0], mine], fsend.at[0, 0], frecv.at[0, 0], partner))
        yield
        o_ref[parts[0][0], mine] = x_ref[...]
        yield
        for part, (span, source, to, steps) in enumerate(parts):
            for step in steps:
                slot = o_ref.at[span, column(at(-step), width)]
                remote(slot, slot, send.at[part, step], recv.at[part, step], partner).wait_recv()
                begin(remote(slot, slot, fsend.at[part, step], frecv.at[part, step], partner))
                if part == 0:
                    yield
        for part, (span, source, to, steps) in enumerate(parts):
            for step in range(chips):
                slot = o_ref.at[span, column(at(-step) + other, width)]
                remote(slot, slot, fsend.at[part, step], frecv.at[part, step], partner).wait_recv()
        for copy in started:
            copy.wait_send()

    return body


def chan_scatter_body(x_ref, o_ref, pair, summed, landed, psend, precv, send, recv):
    tm, chan, core, chips, partner, at = chan_place()
    width = o_ref.shape[1]
    other = 1 - 2 * core
    order = list(range(1, chips)) + [0]
    started = []
    pairs = {}
    for step in order:
        copy = remote(
            x_ref.at[:, column(at(step) + other, width)], pair.at[step], psend.at[step], precv.at[step], partner
        )
        copy.start()
        pairs[step] = copy
    yield
    for step in range(1, chips):
        pairs[step].wait_recv()
        summed[step] = (
            x_ref[:, column(at(step), width)].astype(F32) + pair[step].astype(F32)
        ).astype(summed.dtype)
        copy = remote(summed.at[step], landed.at[step], send.at[step], recv.at[step], (tm, at(step)))
        copy.start()
        started.append(copy)
        yield
    pairs[0].wait_recv()
    o_ref[...] = x_ref[:, column(chan, width)].astype(F32) + pair[0].astype(F32)
    yield
    for copy, step in zip(started, range(1, chips)):
        copy.wait_recv()
        o_ref[...] += landed[step].astype(F32)
    for copy in started:
        copy.wait_send()
    for step in order:
        pairs[step].wait_send()


def share_task(halo, base):
    def body(x_ref, o_ref, send, recv, fsend, frecv):
        tm, chan, core, chips, partner, at = chan_place()
        count = lax.axis_size("tm")
        rows, width = o_ref.shape[0] // count, o_ref.shape[1] // 2
        own = pl.ds(halo, rows)

        def slot(index, half):
            return o_ref.at[pl.ds(pl.multiple_of(index * rows, rows), rows), column(half, width)]

        started = []
        source = x_ref.at[own, pl.ds(pl.multiple_of(base + core * width, width), width)]
        for step in range(1, count):
            copy = remote(source, slot(tm, core), send.at[step], recv.at[step], ((tm + step) % count, chan))
            copy.start()
            started.append(copy)
        yield
        o_ref[pl.ds(pl.multiple_of(tm * rows, rows), rows), :] = x_ref[own, pl.ds(base, 2 * width)]
        yield
        for step in range(1, count):
            landing = slot((tm + count - step) % count, core)
            remote(landing, landing, send.at[step], recv.at[step], partner).wait_recv()
            copy = remote(landing, landing, fsend.at[step], frecv.at[step], partner)
            copy.start()
            started.append(copy)
            yield
        for step in range(1, count):
            landing = slot((tm + count - step) % count, 1 - core)
            remote(landing, landing, send.at[step], frecv.at[step], partner).wait_recv()
        for copy in started:
            copy.wait_send()

    return body


def frames_gather_body(x_ref, o_ref, send, recv):
    tm, chan = lax.axis_index("tm"), lax.axis_index("chan")
    count = lax.axis_size("tm")
    rows = x_ref.shape[0]

    def slot(index):
        return o_ref.at[pl.ds(pl.multiple_of(index * rows, rows), rows)]

    started = []
    for step in range(1, count):
        copy = remote(x_ref, slot(tm), send.at[step], recv.at[step], ((tm + step) % count, chan))
        copy.start()
        started.append(copy)
    yield
    o_ref[pl.ds(pl.multiple_of(tm * rows, rows), rows)] = x_ref[...]
    for turns in range(4):
        yield
    for step in range(1, count):
        landing = slot((tm + count - step) % count)
        remote(landing, landing, send.at[step], recv.at[step], (tm, chan)).wait_recv()
    for copy in started:
        copy.wait_send()


def reduce_body(x_ref, o_ref, landed, send, recv, gsend, grecv):
    tm, chan = lax.axis_index("tm"), lax.axis_index("chan")
    count = lax.axis_size("tm")
    width = x_ref.shape[1] // count
    started = []
    for step in range(1, count):
        to = (tm + step) % count
        copy = remote(x_ref.at[:, column(to, width)], landed.at[step], send.at[step], recv.at[step], (to, chan))
        copy.start()
        started.append(copy)
    yield
    total = x_ref[:, column(tm, width)].astype(F32)
    for step in range(1, count):
        started[step - 1].wait_recv()
        total += landed[step].astype(F32)
    mine = o_ref.at[:, column(tm, width)]
    o_ref[:, column(tm, width)] = total.astype(o_ref.dtype)
    for step in range(1, count):
        copy = remote(mine, mine, gsend.at[step], grecv.at[step], ((tm + step) % count, chan))
        copy.start()
        started.append(copy)
    yield
    yield
    yield
    for step in range(1, count):
        landing = o_ref.at[:, column((tm + count - step) % count, width)]
        remote(landing, landing, send.at[step], grecv.at[step], (tm, chan)).wait_recv()
    for copy in started:
        copy.wait_send()


DMA = pltpu.SemaphoreType.DMA


def chan_gather(value, halo):
    rows, width = value.shape
    chans = lax.axis_size("chan")
    out = jax.ShapeDtypeStruct((rows + 2 * halo, width * chans), value.dtype)
    return (value,), out, [DMA((3, chans // 2))] * 4, chan_gather_task(halo), ("chan", "edge") if halo else ("chan",)


def chan_scatter(value):
    rows, chans = value.shape[0], lax.axis_size("chan")
    width, chips = value.shape[1] // chans, chans // 2
    scratch = [pltpu.VMEM((chips, rows, width), value.dtype)] * 3 + [DMA((chips,))] * 4
    return (value,), jax.ShapeDtypeStruct((rows, width), F32), scratch, chan_scatter_body, ("chan",)


def share(value, halo, part, parts):
    count = lax.axis_size("tm")
    rows, width = value.shape[0] - 2 * halo, value.shape[1] // parts
    out = jax.ShapeDtypeStruct((rows * count, width), value.dtype)
    return (value,), out, [DMA((count,))] * 4, share_task(halo, part * width), ("chan", "tm")


def frames_gather(value):
    count = lax.axis_size("tm")
    out = jax.ShapeDtypeStruct((value.shape[0] * count, value.shape[1]), value.dtype)
    return (value,), out, [DMA((count,))] * 2, frames_gather_body, ("tm",)


def frames_reduce(value):
    count = lax.axis_size("tm")
    landed = pltpu.VMEM((count, value.shape[0], value.shape[1] // count), value.dtype)
    scratch = [landed] + [DMA((count,))] * 4
    return (value,), jax.ShapeDtypeStruct(value.shape, value.dtype), scratch, reduce_body, ("tm",)


def frames_scatter(value):
    count = lax.axis_size("tm")
    rows, width = value.shape[0] // count, value.shape[1]
    scratch = [pltpu.VMEM((count, rows, width), value.dtype)] + [DMA((count,))] * 2
    return (value,), jax.ShapeDtypeStruct((rows, width), F32), scratch, frames_scatter_body, ("tm",)


def expand_body(kernel_ref, mask_ref, o_ref):
    for turns in range(5):
        yield
    rows, width = kernel_ref.shape
    blocks = mask_ref.shape[1]
    spread = (
        lax.broadcasted_iota(jnp.int32, (blocks, width), 1) // (width // blocks)
        == lax.broadcasted_iota(jnp.int32, (blocks, width), 0)
    ).astype(F32).astype(BF16)
    step = 256

    @pl.loop(0, rows // step)
    def _(block):
        span = pl.ds(pl.multiple_of(block * step, step), step)
        keep = jnp.dot(mask_ref[span].astype(F32).astype(BF16), spread, preferred_element_type=F32)
        o_ref[span] = (kernel_ref[span].astype(F32) * keep).astype(o_ref.dtype)

    yield


def expand_task(kernel, mask):
    return (kernel, mask), jax.ShapeDtypeStruct(kernel.shape, kernel.dtype), [], expand_body, ()


def together(number, *tasks):
    axes = set(axis for task in tasks for axis in task[4])
    inputs = [item for task in tasks for item in task[0]]

    def kernel(*refs):
        tm, chan, core, chips, partner, at = chan_place()
        count = lax.axis_size("tm")
        greeted = []
        if "chan" in axes:
            greeted += [partner] + [(tm, at(step)) for step in range(1, chips)]
        if "tm" in axes:
            greeted += [((tm + step) % count, chan) for step in range(1, count)]
        elif "edge" in axes:
            greeted += [((tm + 1) % count, chan), ((tm + count - 1) % count, chan)]
        if "edge" in axes:
            for step in range(1, chips):
                greeted += [((tm + 1) % count, at(step)), ((tm + count - 1) % count, at(step))]
        greet(greeted)
        taken, out, place = 0, len(inputs), len(inputs) + len(tasks)
        bodies = []
        for task in tasks:
            used = refs[taken : taken + len(task[0])] + (refs[out],) + refs[place : place + len(task[2])]
            taken, out, place = taken + len(task[0]), out + 1, place + len(task[2])
            bodies.append(task[3](*used))
        while bodies:
            bodies = [body for body in bodies if next(body, body) is not body]

    whole = pl.BlockSpec(memory_space=pltpu.VMEM)
    return pl.pallas_call(
        kernel,
        out_shape=[task[1] for task in tasks],
        in_specs=[whole] * len(inputs),
        out_specs=[whole] * len(tasks),
        scratch_shapes=[item for task in tasks for item in task[2]],
        compiler_params=pltpu.CompilerParams(
            collective_id=number, has_side_effects=True, vmem_limit_bytes=VMEM_LIMIT
        ),
    )(*inputs)


def taps_kernel(halo, spacing, taps, x_ref, w_ref, ids_ref, alpha_ref, conv_ref, second_ref, spans):
    rows, width = conv_ref.shape
    step = 2 * width
    total = taps * width
    for base in range(0, total, step):
        span = pl.ds(base, min(step, total - base))
        spans[:, span] = lax.dot_general(
            x_ref[...], w_ref[span], (((1,), (1,)), ((), ())), preferred_element_type=F32
        )
    alpha = alpha_ref[...]
    chunk = 128 if rows % 128 == 0 else rows
    for start in range(0, rows, chunk):
        own = ids_ref[pl.ds(start + halo, chunk)]
        conv = jnp.zeros((chunk, width), F32)
        for tap in range(taps):
            window = pl.ds(start + halo + (tap - taps // 2) * spacing, chunk)
            conv = conv + jnp.where(ids_ref[window] == own, spans[window, pl.ds(tap * width, width)], 0.0)
        conv_ref[pl.ds(start, chunk)] = conv
        second_ref[pl.ds(start, chunk)] = snake_act(conv, alpha).astype(second_ref.dtype)


def taps_call(wide, weights, ids, alpha, halo, spacing, taps):
    rows, width = wide.shape[0] - 2 * halo, weights.shape[0] // taps
    whole = pl.BlockSpec(memory_space=pltpu.VMEM)
    return pl.pallas_call(
        functools.partial(taps_kernel, halo, spacing, taps),
        out_shape=[jax.ShapeDtypeStruct((rows, width), F32), jax.ShapeDtypeStruct((rows, width), BF16)],
        in_specs=[whole] * 4,
        out_specs=[whole] * 2,
        scratch_shapes=[pltpu.VMEM((wide.shape[0], weights.shape[0]), F32)],
        compiler_params=pltpu.CompilerParams(vmem_limit_bytes=VMEM_LIMIT),
    )(wide, weights, ids, alpha)


def tap_windows(spacing, taps, grad_ref, mask_ref, flipped, turned):
    rows, width = grad_ref.shape
    chunk, lines = 512, 16

    @pl.loop(0, rows // chunk)
    def _(block):
        part = pl.ds(pl.multiple_of(block * chunk, chunk), chunk)
        flipped[:, part] = grad_ref[part].astype(F32).T

    @pl.loop(0, width // lines)
    def _(block):
        values = flipped[pl.ds(pl.multiple_of(block * lines, lines), lines)]
        for tap in range(taps):
            shift = ((tap - taps // 2) * spacing) % rows
            moved = pltpu.roll(values, shift, 1) if shift else values
            line = pl.multiple_of(tap * width + block * lines, lines)
            turned[pl.ds(line, lines)] = (moved * mask_ref[pl.ds(tap, 1)]).astype(turned.dtype)


def saliency_task(spacing, taps, masks, grads, eff, firsts):
    rows, width = grads.shape

    def body(grad_ref, mask_ref, eff_ref, left_ref, right_ref, o_ref, flipped, turned):
        yield
        tap_windows(spacing, taps, grad_ref, mask_ref, flipped, turned)
        span, step = left_ref.shape[1], 256
        for half, source in enumerate((left_ref, right_ref)):

            @pl.loop(0, span // step)
            def _(block):
                inner = pl.ds(pl.multiple_of(block * step, step), step)
                outer = pl.ds(pl.multiple_of(half * span + block * step, step), step)
                grad = jnp.dot(turned[...], source[:, inner], preferred_element_type=F32)
                o_ref[:, outer] = eff_ref[:, outer].astype(F32) * grad

    scratch = [pltpu.VMEM((width, rows), F32), pltpu.VMEM((taps * width, rows), BF16)]
    return (grads, masks, eff, *firsts), jax.ShapeDtypeStruct(eff.shape, F32), scratch, body, ()


def saliency_kernel(
    spacing, taps, mask_ref, grad_ref, eff_ref, left_ref, right_ref, last_ref, o_ref,
    flipped, turned, eff, first, made, loads, stores, whole_store,
):
    span, step = left_ref.shape[1], 256
    blocks = 2 * span // step
    copies = [
        pltpu.make_async_copy(left_ref, first.at[:, pl.ds(0, span)], loads.at[0]),
        pltpu.make_async_copy(right_ref, first.at[:, pl.ds(span, span)], loads.at[1]),
        pltpu.make_async_copy(eff_ref, eff, loads.at[2]),
    ]
    last = pltpu.make_async_copy(last_ref, o_ref.at[1], whole_store.at[0])
    for copy in copies:
        copy.start()
    last.start()
    tap_windows(spacing, taps, grad_ref, mask_ref, flipped, turned)
    for copy in copies:
        copy.wait()

    def store(slot, block):
        outer = pl.ds(pl.multiple_of(block * step, step), step)
        return pltpu.make_async_copy(made.at[slot], o_ref.at[0, :, outer], stores.at[slot])

    @pl.loop(0, blocks)
    def _(block):
        slot = block % 2
        outer = pl.ds(pl.multiple_of(block * step, step), step)
        grad = jnp.dot(turned[...], first[:, outer], preferred_element_type=F32)

        @pl.when(block >= 2)
        def _():
            store(slot, block).wait()

        made[slot] = eff[:, outer].astype(F32) * grad
        store(slot, block).start()

    for slot in range(2):
        store(slot, slot).wait()
    last.wait()


def saliency(spacing, taps, masks, eff, grads, firsts, last):
    whole, anywhere = pl.BlockSpec(memory_space=pltpu.VMEM), pl.BlockSpec(memory_space=pl.ANY)
    rows, width = grads.shape
    return pl.pallas_call(
        functools.partial(saliency_kernel, spacing, taps),
        out_shape=jax.ShapeDtypeStruct((2,) + eff.shape, F32),
        in_specs=[whole] * 2 + [anywhere] * 4,
        out_specs=anywhere,
        scratch_shapes=[
            pltpu.VMEM((width, rows), F32),
            pltpu.VMEM((taps * width, rows), BF16),
            pltpu.VMEM(eff.shape, BF16),
            pltpu.VMEM((rows, eff.shape[1]), BF16),
            pltpu.VMEM((2, eff.shape[0], 256), F32),
            DMA((3,)),
            DMA((2,)),
            DMA((1,)),
        ],
        compiler_params=pltpu.CompilerParams(vmem_limit_bytes=VMEM_LIMIT),
    )(masks, grads, eff, *firsts, last)


def frames_scatter_body(x_ref, o_ref, landed, send, recv):
    tm, chan = lax.axis_index("tm"), lax.axis_index("chan")
    count = lax.axis_size("tm")
    rows = o_ref.shape[0]
    started = []
    for step in range(1, count):
        to = (tm + step) % count
        copy = remote(
            x_ref.at[pl.ds(pl.multiple_of(to * rows, rows), rows)],
            landed.at[step],
            send.at[step],
            recv.at[step],
            (to, chan),
        )
        copy.start()
        started.append(copy)
    yield
    o_ref[...] = x_ref[pl.ds(pl.multiple_of(tm * rows, rows), rows)].astype(F32)
    for turns in range(4):
        yield
    for step in range(1, count):
        started[step - 1].wait_recv()
        o_ref[...] += landed[step].astype(F32)
    for copy in started:
        copy.wait_send()


def turn_kernel(x_ref, o_ref, send, recv):
    tm, chan = lax.axis_index("tm"), lax.axis_index("chan")
    frames, chans = lax.axis_size("tm"), lax.axis_size("chan")
    ratio = chans // frames
    rows, width = x_ref.shape
    target = chan // ratio
    own = target == tm
    barrier = pltpu.get_barrier_semaphore()
    for frame in range(frames):
        for part in range(ratio):
            source = (frame, tm * ratio + part)

            @pl.when(jnp.logical_or(frame != tm, source[1] != chan))
            def _():
                pl.semaphore_signal(barrier, inc=1, device_id=source, device_id_type=MESH)

    @pl.when(own)
    def _():
        pl.semaphore_wait(barrier, chans - 1)

    @pl.when(jnp.logical_not(own))
    def _():
        pl.semaphore_wait(barrier, chans)

    slot_rows = pl.ds(pl.multiple_of(tm * rows, rows), rows)
    slot_columns = column(chan % ratio, width)
    which = tm * ratio + chan % ratio

    def outgoing(step):
        return remote(
            x_ref,
            o_ref.at[slot_rows, slot_columns],
            send.at[step],
            recv.at[which],
            (target, (chan + step) % chans),
        )

    for step in range(1, chans):
        outgoing(step).start()

    @pl.when(own)
    def _():
        o_ref[slot_rows, slot_columns] = x_ref[...]

    @pl.when(jnp.logical_not(own))
    def _():
        outgoing(0).start()

    for frame in range(frames):
        for part in range(ratio):

            @pl.when(jnp.logical_or(frame != tm, tm * ratio + part != chan))
            def _():
                landing = o_ref.at[pl.ds(frame * rows, rows), pl.ds(part * width, width)]
                remote(
                    landing, landing, send.at[0], recv.at[frame * ratio + part], (tm, chan)
                ).wait_recv()

    for step in range(1, chans):
        outgoing(step).wait_send()

    @pl.when(jnp.logical_not(own))
    def _():
        outgoing(0).wait_send()


def run(kernel, out_shape, dtype, scratch, number, value):
    whole = pl.BlockSpec(memory_space=pltpu.VMEM)
    return pl.pallas_call(
        kernel,
        out_shape=jax.ShapeDtypeStruct(out_shape, dtype),
        in_specs=[whole],
        out_specs=whole,
        scratch_shapes=scratch,
        compiler_params=pltpu.CompilerParams(
            collective_id=number, has_side_effects=True, vmem_limit_bytes=VMEM_LIMIT
        ),
    )(value)


def plain_kernels(*widths):
    return all(width % 128 == 0 for width in widths)


def with_halo(cells, width):
    count = lax.axis_size("tm")
    head, tail = cells[:width], cells[-width:]
    return jnp.concatenate(
        [
            lax.ppermute(tail, "tm", [(i, (i + 1) % count) for i in range(count)]),
            cells,
            lax.ppermute(head, "tm", [((i + 1) % count, i) for i in range(count)]),
        ],
        axis=0,
    )


def turn(value, number):
    frames, chans = lax.axis_size("tm"), lax.axis_size("chan")
    rows, width = value.shape
    if not plain_kernels(width) or chans % frames:
        return lax.all_to_all(
            lax.all_gather(value, "chan", axis=1, tiled=True), "tm", split_axis=1, concat_axis=0, tiled=True
        )
    return run(
        turn_kernel,
        (rows * frames, width * chans // frames),
        value.dtype,
        [pltpu.SemaphoreType.DMA((chans,))] * 2,
        number,
        value,
    )


def snake_act(values, alpha):
    return values + jnp.sin(alpha * values) ** 2 / alpha


def snake_slope(values, alpha):
    return 1.0 + jnp.sin(2.0 * alpha * values)


def track_ids(lengths, frame_index, total_frames):
    starts = jnp.cumsum(lengths) - lengths
    found = jnp.sum((starts[:, None] <= frame_index[None, :]).astype(jnp.int32), axis=0) - 1
    return jnp.where(frame_index < 0, -1, jnp.where(frame_index >= total_frames, -2, found))


def dot_last(left, right):
    return lax.dot_general(left, right, (((1,), (1,)), ((), ())), preferred_element_type=F32)


def dot_first(left, right):
    return lax.dot_general(left, right, (((0,), (0,)), ((), ())), preferred_element_type=F32)


def expand(kernel, mask):
    width, blocks = kernel.shape[-1], mask.shape[-1]
    spread = (
        jnp.arange(width, dtype=jnp.int32)[None, :] // (width // blocks)
        == jnp.arange(blocks, dtype=jnp.int32)[:, None]
    ).astype(BF16)
    keep = jnp.dot(mask.reshape(-1, blocks).astype(BF16), spread, preferred_element_type=F32)
    return (kernel.reshape(-1, width) * keep.astype(BF16)).reshape(kernel.shape)


def per_device(
    latent_input,
    upsample_kernel,
    dilated_kernel,
    pointwise_kernel,
    dilated_prune_mask,
    pointwise_prune_mask,
    snake_freq_upsample,
    snake_freq_dilated,
    snake_freq_pointwise,
    segment_lengths,
    cotangent,
):
    taps, out_local, in_local = upsample_kernel.shape
    stride = taps // 2
    half = stride // 2
    frame_count = latent_input.shape[1]
    rows = frame_count * stride
    tm_count = lax.axis_size("tm")
    tm_index = lax.axis_index("tm")
    total_frames = frame_count * tm_count
    units, kernel_taps, _, channels = dilated_kernel.shape

    def tap_mask(pos, offset):
        own = track_ids(segment_lengths, jnp.floor_divide(pos, stride), total_frames)
        other = track_ids(segment_lengths, jnp.floor_divide(pos + offset, stride), total_frames)
        return (own == other)[:, None]

    row_pos = tm_index * rows + jnp.arange(rows, dtype=jnp.int32)
    frame_pos = jnp.arange(total_frames, dtype=jnp.int32)

    point_eff = expand(pointwise_kernel, pointwise_prune_mask)

    act = snake_act(latent_input.astype(F32), snake_freq_upsample[:, None]).astype(BF16).T
    cot = cotangent.T
    last_parts = jnp.dot(cot, point_eff[units - 1], preferred_element_type=F32).astype(BF16)

    act_all = turn(act, 0)
    product = dot_last(act_all, upsample_kernel.reshape(taps * out_local, in_local)).reshape(
        total_frames, taps, out_local
    )
    frame_ids = track_ids(segment_lengths, frame_pos, total_frames)
    prev_ok = (frame_ids == track_ids(segment_lengths, frame_pos - 1, total_frames))[:, None, None]
    next_ok = (frame_ids == track_ids(segment_lengths, frame_pos + 1, total_frames))[:, None, None]
    low = jnp.pad(product[:-1, half + stride :], ((1, 0), (0, 0), (0, 0)))
    high = jnp.pad(product[1:, :half], ((0, 1), (0, 0), (0, 0)))
    partial = product[:, half : half + stride] + jnp.concatenate(
        [jnp.where(prev_ok, low, 0.0), jnp.where(next_ok, high, 0.0)], axis=1
    )
    partial = partial.astype(BF16).reshape(rows * tm_count, out_local)

    spacings = [3 ** (unit + 1) for unit in range(units)]
    reach = [(kernel_taps // 2) * spacing for spacing in spacings]
    fast = units == 2 and plain_kernels(out_local, channels // 4, channels // tm_count)
    fast = fast and frame_count % 16 == 0 and rows * tm_count % 512 == 0 and units * kernel_taps * out_local % 256 == 0

    def conv_of(first_all, unit, halo):
        spans = dot_last(first_all, flat[unit])
        conv = jnp.zeros((rows, out_local), F32)
        for tap in range(kernel_taps):
            shift = (tap - kernel_taps // 2) * spacings[unit]
            piece = spans[halo + shift : halo + shift + rows, tap * out_local : (tap + 1) * out_local]
            conv = conv + jnp.where(tap_mask(row_pos, shift), piece, 0.0)
        return conv

    def first_of(hidden, unit):
        return snake_act(hidden, snake_freq_dilated[unit]).astype(BF16)

    def second_of(conv, unit):
        return snake_act(conv, snake_freq_pointwise[unit]).astype(BF16)

    def grad_conv_of(grad_second, conv, unit):
        return (grad_second * snake_slope(conv, snake_freq_pointwise[unit])).astype(BF16)

    def spread_back(grad_b, unit):
        return jnp.dot(grad_b, point_eff[unit], preferred_element_type=F32).astype(BF16)

    def shifted_taps(grad_wide, unit, halo):
        pieces = []
        for tap in range(kernel_taps):
            shift = (tap - kernel_taps // 2) * spacings[unit]
            window = grad_wide[halo - shift : halo - shift + rows]
            pieces.append(jnp.where(tap_mask(row_pos, -shift), window, jnp.zeros((), BF16)))
        return jnp.concatenate(pieces, axis=1)

    def outputs(decoded, dil, point_sums):
        return (
            decoded.astype(BF16).T,
            dil.reshape(units, kernel_taps, out_local, channels),
            point_eff.astype(F32) * point_sums.astype(F32),
        )

    if fast:
        halos = [-(-margin // 16) * 16 for margin in reach]
        flat, grad_second_last, hidden = together(
            1,
            expand_task(
                dilated_kernel.reshape(-1, channels),
                dilated_prune_mask.reshape(-1, dilated_prune_mask.shape[-1]),
            ),
            chan_scatter(last_parts),
            frames_scatter(partial),
        )
        flat = flat.reshape(units, kernel_taps * out_local, channels)

        def taps_of(wide, unit):
            pos = tm_index * rows - halos[unit] + jnp.arange(wide.shape[0], dtype=jnp.int32)
            ids = track_ids(segment_lengths, jnp.floor_divide(pos, stride), total_frames).astype(F32)
            ids = jnp.broadcast_to(ids[:, None], (wide.shape[0], out_local))
            alpha = snake_freq_pointwise[unit][None]
            return taps_call(wide, flat[unit], ids, alpha, halos[unit], spacings[unit], kernel_taps)

        (wide0,) = together(2, chan_gather(first_of(hidden, 0), halos[0]))
        conv0, mid0 = taps_of(wide0, 0)
        second0, frames00 = together(3, chan_gather(mid0, 0), share(wide0, halos[0], 0, 2))
        hidden1 = hidden + dot_last(second0, point_eff[0])
        wide1, frames01 = together(
            4, chan_gather(first_of(hidden1, 1), halos[1]), share(wide0, halos[0], 1, 2)
        )
        conv1, mid1 = taps_of(wide1, 1)
        grad_conv1 = grad_conv_of(grad_second_last, conv1, 1)
        grads1, second1 = together(5, frames_gather(grad_conv1), chan_gather(mid1, 0))
        decoded = hidden1 + dot_last(second1, point_eff[1])
        pad = halos[1]
        window = lax.dynamic_slice_in_dim(jnp.pad(grads1, ((pad, pad), (0, 0))), tm_index * rows, rows + 2 * pad, axis=0)
        partial1 = jnp.dot(
            shifted_taps(window, 1, pad), flat[1], preferred_element_type=F32
        ).astype(BF16)
        grad_first, points1, frames10 = together(
            6,
            chan_scatter(partial1),
            frames_reduce(dot_first(cot, second1).astype(BF16)),
            share(wide1, halos[1], 0, 2),
        )
        grad_b0 = (cot.astype(F32) + grad_first * snake_slope(hidden1, snake_freq_dilated[1])).astype(BF16)
        grad_second0, points0, frames11 = together(
            7,
            chan_scatter(spread_back(grad_b0, 0)),
            frames_reduce(dot_first(grad_b0, second0).astype(BF16)),
            share(wide1, halos[1], 1, 2),
        )
        all_pos = jnp.arange(rows * tm_count, dtype=jnp.int32)
        masks = [
            jnp.stack(
                [
                    tap_mask(all_pos, -(tap - kernel_taps // 2) * spacing)[:, 0].astype(F32)
                    for tap in range(kernel_taps)
                ]
            )
            for spacing in spacings
        ]
        grads0, last = together(
            8,
            frames_gather(grad_conv_of(grad_second0, conv0, 0)),
            saliency_task(spacings[1], kernel_taps, masks[1], grads1, flat[1], [frames10, frames11]),
        )
        dil = saliency(spacings[0], kernel_taps, masks[0], flat[0], grads0, [frames00, frames01], last)
        return outputs(decoded, dil, jnp.stack([points0, points1]))

    hidden = lax.psum_scatter(partial, "tm", scatter_dimension=0, tiled=True).astype(F32)
    flat = expand(dilated_kernel, dilated_prune_mask).reshape(units, kernel_taps * out_local, channels)
    saved = []
    for unit in range(units):
        first = first_of(hidden, unit)
        wide = lax.all_gather(with_halo(first, reach[unit]), "chan", axis=1, tiled=True)
        conv = conv_of(wide, unit, reach[unit])
        second = lax.all_gather(second_of(conv, unit), "chan", axis=1, tiled=True)
        saved.append((hidden, wide[reach[unit] : reach[unit] + rows], conv, second))
        hidden = hidden + dot_last(second, point_eff[unit])
    grad_out = cot.astype(F32)
    parts = [None] * (2 * units)
    for unit in reversed(range(units)):
        hidden_in, first_own, conv, second = saved[unit]
        grad_b = grad_out.astype(BF16)
        if unit == units - 1:
            grad_second = lax.psum_scatter(last_parts, "chan", scatter_dimension=1, tiled=True).astype(F32)
        else:
            grad_second = lax.psum_scatter(
                spread_back(grad_b, unit), "chan", scatter_dimension=1, tiled=True
            ).astype(F32)
        grad_conv = grad_conv_of(grad_second, conv, unit)
        shifted = shifted_taps(with_halo(grad_conv, reach[unit]), unit, reach[unit])
        parts[unit] = dot_first(shifted, first_own).astype(BF16)
        parts[units + unit] = dot_first(grad_b, second).astype(BF16)
        if unit > 0:
            back = jnp.dot(shifted, flat[unit], preferred_element_type=F32).astype(BF16)
            grad_first = lax.psum_scatter(back, "chan", scatter_dimension=1, tiled=True).astype(F32)
            grad_out = grad_out + grad_first * snake_slope(hidden_in, snake_freq_dilated[unit])
    sums = lax.psum(parts, "tm")
    dil = flat.astype(F32) * jnp.stack(sums[:units]).astype(F32)
    return outputs(hidden, dil, jnp.stack(sums[units:]))


def solution(mesh):
    return jax.shard_map(
        per_device,
        mesh=mesh,
        in_specs=(
            P("chan", "tm"),
            P(None, "chan", "tm"),
            P(None, None, "chan", None),
            P(None, "chan", None),
            P(None, None, "chan", None),
            P(None, "chan", None),
            P("chan"),
            P(None, "chan"),
            P(None, "chan"),
            P(),
            P("chan", "tm"),
        ),
        out_specs=(P("chan", "tm"), P(None, None, "chan", None), P(None, "chan", None)),
        check_vma=False,
    )
```

```python
import functools

import jax
import jax.numpy as jnp
from jax import lax
from jax.experimental import pallas as pl
from jax.experimental.pallas import tpu as pltpu
from jax.sharding import PartitionSpec as P

MESH = pl.DeviceIdType.MESH
BF16 = jnp.bfloat16
F32 = jnp.float32
VMEM_LIMIT = 48 * 1024 * 1024


def remote(src, dst, send, recv, device):
    return pltpu.make_async_remote_copy(
        src_ref=src, dst_ref=dst, send_sem=send, recv_sem=recv, device_id=device, device_id_type=MESH
    )


def greet(devices):
    barrier = pltpu.get_barrier_semaphore()
    for device in devices:
        pl.semaphore_signal(barrier, inc=1, device_id=device, device_id_type=MESH)
    pl.semaphore_wait(barrier, len(devices))


def chan_place():
    tm, chan = lax.axis_index("tm"), lax.axis_index("chan")
    chips = lax.axis_size("chan") // 2
    chip, core = chan // 2, chan % 2
    partner = (tm, chan + 1 - 2 * core)

    def at(step):
        return ((chip + step + chips) % chips) * 2 + core

    return tm, chan, core, chips, partner, at


def column(index, width):
    return pl.ds(pl.multiple_of(index * width, width), width)


def chan_gather_task(halo):
    def body(x_ref, o_ref, send, recv, fsend, frecv):
        tm, chan, core, chips, partner, at = chan_place()
        frames = lax.axis_size("tm")
        rows, width = x_ref.shape
        mine = column(chan, width)
        other = 1 - 2 * core
        parts = [(pl.ds(halo, rows), x_ref, tm, range(1, chips))]
        if halo:
            parts += [
                (pl.ds(0, halo), x_ref.at[pl.ds(rows - halo, halo)], (tm + 1) % frames, range(chips)),
                (pl.ds(halo + rows, halo), x_ref.at[pl.ds(0, halo)], (tm + frames - 1) % frames, range(chips)),
            ]
        started = []

        def begin(copy):
            copy.start()
            started.append(copy)

        for part, (span, source, to, steps) in reversed(list(enumerate(parts))):
            for step in steps:
                begin(remote(source, o_ref.at[span, mine], send.at[part, step], recv.at[part, step], (to, at(step))))
        begin(remote(x_ref, o_ref.at[parts[0][0], mine], fsend.at[0, 0], frecv.at[0, 0], partner))
        yield
        o_ref[parts[0][0], mine] = x_ref[...]
        yield
        for part, (span, source, to, steps) in enumerate(parts):
            for step in steps:
                slot = o_ref.at[span, column(at(-step), width)]
                remote(slot, slot, send.at[part, step], recv.at[part, step], partner).wait_recv()
                begin(remote(slot, slot, fsend.at[part, step], frecv.at[part, step], partner))
                if part == 0:
                    yield
        for part, (span, source, to, steps) in enumerate(parts):
            for step in range(chips):
                slot = o_ref.at[span, column(at(-step) + other, width)]
                remote(slot, slot, fsend.at[part, step], frecv.at[part, step], partner).wait_recv()
        for copy in started:
            copy.wait_send()

    return body


def chan_scatter_body(x_ref, o_ref, pair, summed, landed, psend, precv, send, recv):
    tm, chan, core, chips, partner, at = chan_place()
    width = o_ref.shape[1]
    other = 1 - 2 * core
    order = list(range(1, chips)) + [0]
    started = []
    pairs = {}
    for step in order:
        copy = remote(
            x_ref.at[:, column(at(step) + other, width)], pair.at[step], psend.at[step], precv.at[step], partner
        )
        copy.start()
        pairs[step] = copy
    yield
    for step in range(1, chips):
        pairs[step].wait_recv()
        summed[step] = (
            x_ref[:, column(at(step), width)].astype(F32) + pair[step].astype(F32)
        ).astype(summed.dtype)
        copy = remote(summed.at[step], landed.at[step], send.at[step], recv.at[step], (tm, at(step)))
        copy.start()
        started.append(copy)
    pairs[0].wait_recv()
    o_ref[...] = x_ref[:, column(chan, width)].astype(F32) + pair[0].astype(F32)
    for turns in range(4):
        yield
    for copy, step in zip(started, range(1, chips)):
        copy.wait_recv()
        o_ref[...] += landed[step].astype(F32)
    for copy in started:
        copy.wait_send()
    for step in order:
        pairs[step].wait_send()


def share_task(halo, base):
    def body(x_ref, o_ref, send, recv, fsend, frecv):
        tm, chan, core, chips, partner, at = chan_place()
        count = lax.axis_size("tm")
        rows, width = o_ref.shape[0] // count, o_ref.shape[1] // 2
        own = pl.ds(halo, rows)

        def slot(index, half):
            return o_ref.at[pl.ds(pl.multiple_of(index * rows, rows), rows), column(half, width)]

        started = []
        source = x_ref.at[own, pl.ds(pl.multiple_of(base + core * width, width), width)]
        for step in range(1, count):
            copy = remote(source, slot(tm, core), send.at[step], recv.at[step], ((tm + step) % count, chan))
            copy.start()
            started.append(copy)
        yield
        o_ref[pl.ds(pl.multiple_of(tm * rows, rows), rows), :] = x_ref[own, pl.ds(base, 2 * width)]
        yield
        for step in range(1, count):
            landing = slot((tm + count - step) % count, core)
            remote(landing, landing, send.at[step], recv.at[step], partner).wait_recv()
            copy = remote(landing, landing, fsend.at[step], frecv.at[step], partner)
            copy.start()
            started.append(copy)
            yield
        for step in range(1, count):
            landing = slot((tm + count - step) % count, 1 - core)
            remote(landing, landing, send.at[step], frecv.at[step], partner).wait_recv()
        for copy in started:
            copy.wait_send()

    return body


def frames_gather_body(x_ref, o_ref, send, recv):
    tm, chan = lax.axis_index("tm"), lax.axis_index("chan")
    count = lax.axis_size("tm")
    rows = x_ref.shape[0]

    def slot(index):
        return o_ref.at[pl.ds(pl.multiple_of(index * rows, rows), rows)]

    started = []
    for step in range(1, count):
        copy = remote(x_ref, slot(tm), send.at[step], recv.at[step], ((tm + step) % count, chan))
        copy.start()
        started.append(copy)
    yield
    o_ref[pl.ds(pl.multiple_of(tm * rows, rows), rows)] = x_ref[...]
    for turns in range(4):
        yield
    for step in range(1, count):
        landing = slot((tm + count - step) % count)
        remote(landing, landing, send.at[step], recv.at[step], (tm, chan)).wait_recv()
    for copy in started:
        copy.wait_send()


def reduce_body(x_ref, o_ref, landed, send, recv, gsend, grecv):
    tm, chan = lax.axis_index("tm"), lax.axis_index("chan")
    count = lax.axis_size("tm")
    width = x_ref.shape[1] // count
    started = []
    for step in range(1, count):
        to = (tm + step) % count
        copy = remote(x_ref.at[:, column(to, width)], landed.at[step], send.at[step], recv.at[step], (to, chan))
        copy.start()
        started.append(copy)
    yield
    total = x_ref[:, column(tm, width)].astype(F32)
    for step in range(1, count):
        started[step - 1].wait_recv()
        total += landed[step].astype(F32)
    mine = o_ref.at[:, column(tm, width)]
    o_ref[:, column(tm, width)] = total.astype(o_ref.dtype)
    for step in range(1, count):
        copy = remote(mine, mine, gsend.at[step], grecv.at[step], ((tm + step) % count, chan))
        copy.start()
        started.append(copy)
    yield
    yield
    yield
    for step in range(1, count):
        landing = o_ref.at[:, column((tm + count - step) % count, width)]
        remote(landing, landing, send.at[step], grecv.at[step], (tm, chan)).wait_recv()
    for copy in started:
        copy.wait_send()


DMA = pltpu.SemaphoreType.DMA


def chan_gather(value, halo):
    rows, width = value.shape
    chans = lax.axis_size("chan")
    out = jax.ShapeDtypeStruct((rows + 2 * halo, width * chans), value.dtype)
    return (value,), out, [DMA((3, chans // 2))] * 4, chan_gather_task(halo), ("chan", "edge") if halo else ("chan",)


def chan_scatter(value):
    rows, chans = value.shape[0], lax.axis_size("chan")
    width, chips = value.shape[1] // chans, chans // 2
    scratch = [pltpu.VMEM((chips, rows, width), value.dtype)] * 3 + [DMA((chips,))] * 4
    return (value,), jax.ShapeDtypeStruct((rows, width), F32), scratch, chan_scatter_body, ("chan",)


def share(value, halo, part, parts):
    count = lax.axis_size("tm")
    rows, width = value.shape[0] - 2 * halo, value.shape[1] // parts
    out = jax.ShapeDtypeStruct((rows * count, width), value.dtype)
    return (value,), out, [DMA((count,))] * 4, share_task(halo, part * width), ("chan", "tm")


def frames_gather(value):
    count = lax.axis_size("tm")
    out = jax.ShapeDtypeStruct((value.shape[0] * count, value.shape[1]), value.dtype)
    return (value,), out, [DMA((count,))] * 2, frames_gather_body, ("tm",)


def frames_reduce(value):
    count = lax.axis_size("tm")
    landed = pltpu.VMEM((count, value.shape[0], value.shape[1] // count), value.dtype)
    scratch = [landed] + [DMA((count,))] * 4
    return (value,), jax.ShapeDtypeStruct(value.shape, value.dtype), scratch, reduce_body, ("tm",)


def frames_scatter(value):
    count = lax.axis_size("tm")
    rows, width = value.shape[0] // count, value.shape[1]
    scratch = [pltpu.VMEM((count, rows, width), value.dtype)] + [DMA((count,))] * 2
    return (value,), jax.ShapeDtypeStruct((rows, width), F32), scratch, frames_scatter_body, ("tm",)


def expand_body(kernel_ref, mask_ref, o_ref):
    for turns in range(5):
        yield
    rows, width = kernel_ref.shape
    blocks = mask_ref.shape[1]
    spread = (
        lax.broadcasted_iota(jnp.int32, (blocks, width), 1) // (width // blocks)
        == lax.broadcasted_iota(jnp.int32, (blocks, width), 0)
    ).astype(F32).astype(BF16)
    step = 256

    @pl.loop(0, rows // step)
    def _(block):
        span = pl.ds(pl.multiple_of(block * step, step), step)
        keep = jnp.dot(mask_ref[span].astype(F32).astype(BF16), spread, preferred_element_type=F32)
        o_ref[span] = (kernel_ref[span].astype(F32) * keep).astype(o_ref.dtype)

    yield


def expand_task(kernel, mask):
    return (kernel, mask), jax.ShapeDtypeStruct(kernel.shape, kernel.dtype), [], expand_body, ()


def together(number, *tasks):
    axes = set(axis for task in tasks for axis in task[4])
    inputs = [item for task in tasks for item in task[0]]

    def kernel(*refs):
        tm, chan, core, chips, partner, at = chan_place()
        count = lax.axis_size("tm")
        greeted = []
        if "chan" in axes:
            greeted += [partner] + [(tm, at(step)) for step in range(1, chips)]
        if "tm" in axes:
            greeted += [((tm + step) % count, chan) for step in range(1, count)]
        elif "edge" in axes:
            greeted += [((tm + 1) % count, chan), ((tm + count - 1) % count, chan)]
        if "edge" in axes:
            for step in range(1, chips):
                greeted += [((tm + 1) % count, at(step)), ((tm + count - 1) % count, at(step))]
        greet(greeted)
        taken, out, place = 0, len(inputs), len(inputs) + len(tasks)
        bodies = []
        for task in tasks:
            used = refs[taken : taken + len(task[0])] + (refs[out],) + refs[place : place + len(task[2])]
            taken, out, place = taken + len(task[0]), out + 1, place + len(task[2])
            bodies.append(task[3](*used))
        while bodies:
            bodies = [body for body in bodies if next(body, body) is not body]

    whole = pl.BlockSpec(memory_space=pltpu.VMEM)
    return pl.pallas_call(
        kernel,
        out_shape=[task[1] for task in tasks],
        in_specs=[whole] * len(inputs),
        out_specs=[whole] * len(tasks),
        scratch_shapes=[item for task in tasks for item in task[2]],
        compiler_params=pltpu.CompilerParams(
            collective_id=number, has_side_effects=True, vmem_limit_bytes=VMEM_LIMIT
        ),
    )(*inputs)


def taps_kernel(halo, spacing, taps, x_ref, w_ref, ids_ref, alpha_ref, conv_ref, second_ref, spans):
    rows, width = conv_ref.shape
    step = 2 * width
    total = taps * width
    for base in range(0, total, step):
        span = pl.ds(base, min(step, total - base))
        spans[:, span] = lax.dot_general(
            x_ref[...], w_ref[span], (((1,), (1,)), ((), ())), preferred_element_type=F32
        )
    alpha = alpha_ref[...]
    chunk = 128 if rows % 128 == 0 else rows
    for start in range(0, rows, chunk):
        own = ids_ref[pl.ds(start + halo, chunk)]
        conv = jnp.zeros((chunk, width), F32)
        for tap in range(taps):
            window = pl.ds(start + halo + (tap - taps // 2) * spacing, chunk)
            conv = conv + jnp.where(ids_ref[window] == own, spans[window, pl.ds(tap * width, width)], 0.0)
        conv_ref[pl.ds(start, chunk)] = conv
        second_ref[pl.ds(start, chunk)] = snake_act(conv, alpha).astype(second_ref.dtype)


def taps_call(wide, weights, ids, alpha, halo, spacing, taps):
    rows, width = wide.shape[0] - 2 * halo, weights.shape[0] // taps
    whole = pl.BlockSpec(memory_space=pltpu.VMEM)
    return pl.pallas_call(
        functools.partial(taps_kernel, halo, spacing, taps),
        out_shape=[jax.ShapeDtypeStruct((rows, width), F32), jax.ShapeDtypeStruct((rows, width), BF16)],
        in_specs=[whole] * 4,
        out_specs=[whole] * 2,
        scratch_shapes=[pltpu.VMEM((wide.shape[0], weights.shape[0]), F32)],
        compiler_params=pltpu.CompilerParams(vmem_limit_bytes=VMEM_LIMIT),
    )(wide, weights, ids, alpha)


def tap_windows(spacing, taps, grad_ref, mask_ref, flipped, turned):
    rows, width = grad_ref.shape
    chunk, lines = 512, 16

    @pl.loop(0, rows // chunk)
    def _(block):
        part = pl.ds(pl.multiple_of(block * chunk, chunk), chunk)
        flipped[:, part] = grad_ref[part].astype(F32).T

    @pl.loop(0, width // lines)
    def _(block):
        values = flipped[pl.ds(pl.multiple_of(block * lines, lines), lines)]
        for tap in range(taps):
            shift = ((tap - taps // 2) * spacing) % rows
            moved = pltpu.roll(values, shift, 1) if shift else values
            line = pl.multiple_of(tap * width + block * lines, lines)
            turned[pl.ds(line, lines)] = (moved * mask_ref[pl.ds(tap, 1)]).astype(turned.dtype)


def saliency_task(spacing, taps, masks, grads, eff, firsts):
    rows, width = grads.shape

    def body(grad_ref, mask_ref, eff_ref, left_ref, right_ref, o_ref, flipped, turned):
        yield
        tap_windows(spacing, taps, grad_ref, mask_ref, flipped, turned)
        span, step = left_ref.shape[1], 256
        for half, source in enumerate((left_ref, right_ref)):

            @pl.loop(0, span // step)
            def _(block):
                inner = pl.ds(pl.multiple_of(block * step, step), step)
                outer = pl.ds(pl.multiple_of(half * span + block * step, step), step)
                grad = jnp.dot(turned[...], source[:, inner], preferred_element_type=F32)
                o_ref[:, outer] = eff_ref[:, outer].astype(F32) * grad

    scratch = [pltpu.VMEM((width, rows), F32), pltpu.VMEM((taps * width, rows), BF16)]
    return (grads, masks, eff, *firsts), jax.ShapeDtypeStruct(eff.shape, F32), scratch, body, ()


def saliency_kernel(
    spacing, taps, mask_ref, grad_ref, eff_ref, left_ref, right_ref, last_ref, o_ref,
    flipped, turned, eff, first, made, loads, stores, whole_store,
):
    span, step = left_ref.shape[1], 256
    blocks = 2 * span // step
    copies = [
        pltpu.make_async_copy(left_ref, first.at[:, pl.ds(0, span)], loads.at[0]),
        pltpu.make_async_copy(right_ref, first.at[:, pl.ds(span, span)], loads.at[1]),
        pltpu.make_async_copy(eff_ref, eff, loads.at[2]),
    ]
    last = pltpu.make_async_copy(last_ref, o_ref.at[1], whole_store.at[0])
    for copy in copies:
        copy.start()
    last.start()
    tap_windows(spacing, taps, grad_ref, mask_ref, flipped, turned)
    for copy in copies:
        copy.wait()

    def store(slot, block):
        outer = pl.ds(pl.multiple_of(block * step, step), step)
        return pltpu.make_async_copy(made.at[slot], o_ref.at[0, :, outer], stores.at[slot])

    @pl.loop(0, blocks)
    def _(block):
        slot = block % 2
        outer = pl.ds(pl.multiple_of(block * step, step), step)
        grad = jnp.dot(turned[...], first[:, outer], preferred_element_type=F32)

        @pl.when(block >= 2)
        def _():
            store(slot, block).wait()

        made[slot] = eff[:, outer].astype(F32) * grad
        store(slot, block).start()

    for slot in range(2):
        store(slot, slot).wait()
    last.wait()


def saliency(spacing, taps, masks, eff, grads, firsts, last):
    whole, anywhere = pl.BlockSpec(memory_space=pltpu.VMEM), pl.BlockSpec(memory_space=pl.ANY)
    rows, width = grads.shape
    return pl.pallas_call(
        functools.partial(saliency_kernel, spacing, taps),
        out_shape=jax.ShapeDtypeStruct((2,) + eff.shape, F32),
        in_specs=[whole] * 2 + [anywhere] * 3 + [whole],
        out_specs=anywhere,
        scratch_shapes=[
            pltpu.VMEM((width, rows), F32),
            pltpu.VMEM((taps * width, rows), BF16),
            pltpu.VMEM(eff.shape, BF16),
            pltpu.VMEM((rows, eff.shape[1]), BF16),
            pltpu.VMEM((2, eff.shape[0], 256), F32),
            DMA((3,)),
            DMA((2,)),
            DMA((1,)),
        ],
        compiler_params=pltpu.CompilerParams(vmem_limit_bytes=VMEM_LIMIT),
    )(masks, grads, eff, *firsts, last)


def frames_scatter_body(x_ref, o_ref, landed, send, recv):
    tm, chan = lax.axis_index("tm"), lax.axis_index("chan")
    count = lax.axis_size("tm")
    rows = o_ref.shape[0]
    started = []
    for step in range(1, count):
        to = (tm + step) % count
        copy = remote(
            x_ref.at[pl.ds(pl.multiple_of(to * rows, rows), rows)],
            landed.at[step],
            send.at[step],
            recv.at[step],
            (to, chan),
        )
        copy.start()
        started.append(copy)
    yield
    o_ref[...] = x_ref[pl.ds(pl.multiple_of(tm * rows, rows), rows)].astype(F32)
    for turns in range(4):
        yield
    for step in range(1, count):
        started[step - 1].wait_recv()
        o_ref[...] += landed[step].astype(F32)
    for copy in started:
        copy.wait_send()


def turn_kernel(x_ref, o_ref, send, recv):
    tm, chan = lax.axis_index("tm"), lax.axis_index("chan")
    frames, chans = lax.axis_size("tm"), lax.axis_size("chan")
    ratio = chans // frames
    rows, width = x_ref.shape
    target = chan // ratio
    own = target == tm
    barrier = pltpu.get_barrier_semaphore()
    for frame in range(frames):
        for part in range(ratio):
            source = (frame, tm * ratio + part)

            @pl.when(jnp.logical_or(frame != tm, source[1] != chan))
            def _():
                pl.semaphore_signal(barrier, inc=1, device_id=source, device_id_type=MESH)

    @pl.when(own)
    def _():
        pl.semaphore_wait(barrier, chans - 1)

    @pl.when(jnp.logical_not(own))
    def _():
        pl.semaphore_wait(barrier, chans)

    slot_rows = pl.ds(pl.multiple_of(tm * rows, rows), rows)
    slot_columns = column(chan % ratio, width)
    which = tm * ratio + chan % ratio

    def outgoing(step):
        return remote(
            x_ref,
            o_ref.at[slot_rows, slot_columns],
            send.at[step],
            recv.at[which],
            (target, (chan + step) % chans),
        )

    for step in range(1, chans):
        outgoing(step).start()

    @pl.when(own)
    def _():
        o_ref[slot_rows, slot_columns] = x_ref[...]

    @pl.when(jnp.logical_not(own))
    def _():
        outgoing(0).start()

    for frame in range(frames):
        for part in range(ratio):

            @pl.when(jnp.logical_or(frame != tm, tm * ratio + part != chan))
            def _():
                landing = o_ref.at[pl.ds(frame * rows, rows), pl.ds(part * width, width)]
                remote(
                    landing, landing, send.at[0], recv.at[frame * ratio + part], (tm, chan)
                ).wait_recv()

    for step in range(1, chans):
        outgoing(step).wait_send()

    @pl.when(jnp.logical_not(own))
    def _():
        outgoing(0).wait_send()


def run(kernel, out_shape, dtype, scratch, number, value):
    whole = pl.BlockSpec(memory_space=pltpu.VMEM)
    return pl.pallas_call(
        kernel,
        out_shape=jax.ShapeDtypeStruct(out_shape, dtype),
        in_specs=[whole],
        out_specs=whole,
        scratch_shapes=scratch,
        compiler_params=pltpu.CompilerParams(
            collective_id=number, has_side_effects=True, vmem_limit_bytes=VMEM_LIMIT
        ),
    )(value)


def plain_kernels(*widths):
    return all(width % 128 == 0 for width in widths)


def with_halo(cells, width):
    count = lax.axis_size("tm")
    head, tail = cells[:width], cells[-width:]
    return jnp.concatenate(
        [
            lax.ppermute(tail, "tm", [(i, (i + 1) % count) for i in range(count)]),
            cells,
            lax.ppermute(head, "tm", [((i + 1) % count, i) for i in range(count)]),
        ],
        axis=0,
    )


def turn(value, number):
    frames, chans = lax.axis_size("tm"), lax.axis_size("chan")
    rows, width = value.shape
    if not plain_kernels(width) or chans % frames:
        return lax.all_to_all(
            lax.all_gather(value, "chan", axis=1, tiled=True), "tm", split_axis=1, concat_axis=0, tiled=True
        )
    return run(
        turn_kernel,
        (rows * frames, width * chans // frames),
        value.dtype,
        [pltpu.SemaphoreType.DMA((chans,))] * 2,
        number,
        value,
    )


def snake_act(values, alpha):
    return values + jnp.sin(alpha * values) ** 2 / alpha


def snake_slope(values, alpha):
    return 1.0 + jnp.sin(2.0 * alpha * values)


def track_ids(lengths, frame_index, total_frames):
    starts = jnp.cumsum(lengths) - lengths
    found = jnp.sum((starts[:, None] <= frame_index[None, :]).astype(jnp.int32), axis=0) - 1
    return jnp.where(frame_index < 0, -1, jnp.where(frame_index >= total_frames, -2, found))


def dot_last(left, right):
    return lax.dot_general(left, right, (((1,), (1,)), ((), ())), preferred_element_type=F32)


def dot_first(left, right):
    return lax.dot_general(left, right, (((0,), (0,)), ((), ())), preferred_element_type=F32)


def expand(kernel, mask):
    width, blocks = kernel.shape[-1], mask.shape[-1]
    spread = (
        jnp.arange(width, dtype=jnp.int32)[None, :] // (width // blocks)
        == jnp.arange(blocks, dtype=jnp.int32)[:, None]
    ).astype(BF16)
    keep = jnp.dot(mask.reshape(-1, blocks).astype(BF16), spread, preferred_element_type=F32)
    return (kernel.reshape(-1, width) * keep.astype(BF16)).reshape(kernel.shape)


def per_device(
    latent_input,
    upsample_kernel,
    dilated_kernel,
    pointwise_kernel,
    dilated_prune_mask,
    pointwise_prune_mask,
    snake_freq_upsample,
    snake_freq_dilated,
    snake_freq_pointwise,
    segment_lengths,
    cotangent,
):
    taps, out_local, in_local = upsample_kernel.shape
    stride = taps // 2
    half = stride // 2
    frame_count = latent_input.shape[1]
    rows = frame_count * stride
    tm_count = lax.axis_size("tm")
    tm_index = lax.axis_index("tm")
    total_frames = frame_count * tm_count
    units, kernel_taps, _, channels = dilated_kernel.shape

    def tap_mask(pos, offset):
        own = track_ids(segment_lengths, jnp.floor_divide(pos, stride), total_frames)
        other = track_ids(segment_lengths, jnp.floor_divide(pos + offset, stride), total_frames)
        return (own == other)[:, None]

    row_pos = tm_index * rows + jnp.arange(rows, dtype=jnp.int32)
    frame_pos = jnp.arange(total_frames, dtype=jnp.int32)

    point_eff = expand(pointwise_kernel, pointwise_prune_mask)

    act = snake_act(latent_input.astype(F32), snake_freq_upsample[:, None]).astype(BF16).T
    cot = cotangent.T
    last_parts = jnp.dot(cot, point_eff[units - 1], preferred_element_type=F32).astype(BF16)

    act_all = turn(act, 0)
    product = dot_last(act_all, upsample_kernel.reshape(taps * out_local, in_local)).reshape(
        total_frames, taps, out_local
    )
    frame_ids = track_ids(segment_lengths, frame_pos, total_frames)
    prev_ok = (frame_ids == track_ids(segment_lengths, frame_pos - 1, total_frames))[:, None, None]
    next_ok = (frame_ids == track_ids(segment_lengths, frame_pos + 1, total_frames))[:, None, None]
    low = jnp.pad(product[:-1, half + stride :], ((1, 0), (0, 0), (0, 0)))
    high = jnp.pad(product[1:, :half], ((0, 1), (0, 0), (0, 0)))
    partial = product[:, half : half + stride] + jnp.concatenate(
        [jnp.where(prev_ok, low, 0.0), jnp.where(next_ok, high, 0.0)], axis=1
    )
    partial = partial.astype(BF16).reshape(rows * tm_count, out_local)

    spacings = [3 ** (unit + 1) for unit in range(units)]
    reach = [(kernel_taps // 2) * spacing for spacing in spacings]
    fast = units == 2 and plain_kernels(out_local, channels // 4, channels // tm_count)
    fast = fast and frame_count % 16 == 0 and rows * tm_count % 512 == 0 and units * kernel_taps * out_local % 256 == 0

    def conv_of(first_all, unit, halo):
        spans = dot_last(first_all, flat[unit])
        conv = jnp.zeros((rows, out_local), F32)
        for tap in range(kernel_taps):
            shift = (tap - kernel_taps // 2) * spacings[unit]
            piece = spans[halo + shift : halo + shift + rows, tap * out_local : (tap + 1) * out_local]
            conv = conv + jnp.where(tap_mask(row_pos, shift), piece, 0.0)
        return conv

    def first_of(hidden, unit):
        return snake_act(hidden, snake_freq_dilated[unit]).astype(BF16)

    def second_of(conv, unit):
        return snake_act(conv, snake_freq_pointwise[unit]).astype(BF16)

    def grad_conv_of(grad_second, conv, unit):
        return (grad_second * snake_slope(conv, snake_freq_pointwise[unit])).astype(BF16)

    def spread_back(grad_b, unit):
        return jnp.dot(grad_b, point_eff[unit], preferred_element_type=F32).astype(BF16)

    def shifted_taps(grad_wide, unit, halo):
        pieces = []
        for tap in range(kernel_taps):
            shift = (tap - kernel_taps // 2) * spacings[unit]
            window = grad_wide[halo - shift : halo - shift + rows]
            pieces.append(jnp.where(tap_mask(row_pos, -shift), window, jnp.zeros((), BF16)))
        return jnp.concatenate(pieces, axis=1)

    def outputs(decoded, dil, point_sums):
        return (
            decoded.astype(BF16).T,
            dil.reshape(units, kernel_taps, out_local, channels),
            point_eff.astype(F32) * point_sums.astype(F32),
        )

    if fast:
        halos = [-(-margin // 16) * 16 for margin in reach]
        flat, grad_second_last, hidden = together(
            1,
            expand_task(
                dilated_kernel.reshape(-1, channels),
                dilated_prune_mask.reshape(-1, dilated_prune_mask.shape[-1]),
            ),
            chan_scatter(last_parts),
            frames_scatter(partial),
        )
        flat = flat.reshape(units, kernel_taps * out_local, channels)

        def taps_of(wide, unit):
            pos = tm_index * rows - halos[unit] + jnp.arange(wide.shape[0], dtype=jnp.int32)
            ids = track_ids(segment_lengths, jnp.floor_divide(pos, stride), total_frames).astype(F32)
            ids = jnp.broadcast_to(ids[:, None], (wide.shape[0], out_local))
            alpha = snake_freq_pointwise[unit][None]
            return taps_call(wide, flat[unit], ids, alpha, halos[unit], spacings[unit], kernel_taps)

        (wide0,) = together(2, chan_gather(first_of(hidden, 0), halos[0]))
        conv0, mid0 = taps_of(wide0, 0)
        second0, frames00 = together(3, chan_gather(mid0, 0), share(wide0, halos[0], 0, 2))
        hidden1 = hidden + dot_last(second0, point_eff[0])
        wide1, frames01 = together(
            4, chan_gather(first_of(hidden1, 1), halos[1]), share(wide0, halos[0], 1, 2)
        )
        conv1, mid1 = taps_of(wide1, 1)
        grad_conv1 = grad_conv_of(grad_second_last, conv1, 1)
        grads1, second1 = together(5, frames_gather(grad_conv1), chan_gather(mid1, 0))
        decoded = hidden1 + dot_last(second1, point_eff[1])
        pad = halos[1]
        window = lax.dynamic_slice_in_dim(jnp.pad(grads1, ((pad, pad), (0, 0))), tm_index * rows, rows + 2 * pad, axis=0)
        partial1 = jnp.dot(
            shifted_taps(window, 1, pad), flat[1], preferred_element_type=F32
        ).astype(BF16)
        grad_first, points1, frames10 = together(
            6,
            chan_scatter(partial1),
            frames_reduce(dot_first(cot, second1).astype(BF16)),
            share(wide1, halos[1], 0, 2),
        )
        grad_b0 = (cot.astype(F32) + grad_first * snake_slope(hidden1, snake_freq_dilated[1])).astype(BF16)
        grad_second0, points0, frames11 = together(
            7,
            chan_scatter(spread_back(grad_b0, 0)),
            frames_reduce(dot_first(grad_b0, second0).astype(BF16)),
            share(wide1, halos[1], 1, 2),
        )
        all_pos = jnp.arange(rows * tm_count, dtype=jnp.int32)
        masks = [
            jnp.stack(
                [
                    tap_mask(all_pos, -(tap - kernel_taps // 2) * spacing)[:, 0].astype(F32)
                    for tap in range(kernel_taps)
                ]
            )
            for spacing in spacings
        ]
        grads0, last = together(
            8,
            frames_gather(grad_conv_of(grad_second0, conv0, 0)),
            saliency_task(spacings[1], kernel_taps, masks[1], grads1, flat[1], [frames10, frames11]),
        )
        dil = saliency(spacings[0], kernel_taps, masks[0], flat[0], grads0, [frames00, frames01], last)
        return outputs(decoded, dil, jnp.stack([points0, points1]))

    hidden = lax.psum_scatter(partial, "tm", scatter_dimension=0, tiled=True).astype(F32)
    flat = expand(dilated_kernel, dilated_prune_mask).reshape(units, kernel_taps * out_local, channels)
    saved = []
    for unit in range(units):
        first = first_of(hidden, unit)
        wide = lax.all_gather(with_halo(first, reach[unit]), "chan", axis=1, tiled=True)
        conv = conv_of(wide, unit, reach[unit])
        second = lax.all_gather(second_of(conv, unit), "chan", axis=1, tiled=True)
        saved.append((hidden, wide[reach[unit] : reach[unit] + rows], conv, second))
        hidden = hidden + dot_last(second, point_eff[unit])
    grad_out = cot.astype(F32)
    parts = [None] * (2 * units)
    for unit in reversed(range(units)):
        hidden_in, first_own, conv, second = saved[unit]
        grad_b = grad_out.astype(BF16)
        if unit == units - 1:
            grad_second = lax.psum_scatter(last_parts, "chan", scatter_dimension=1, tiled=True).astype(F32)
        else:
            grad_second = lax.psum_scatter(
                spread_back(grad_b, unit), "chan", scatter_dimension=1, tiled=True
            ).astype(F32)
        grad_conv = grad_conv_of(grad_second, conv, unit)
        shifted = shifted_taps(with_halo(grad_conv, reach[unit]), unit, reach[unit])
        parts[unit] = dot_first(shifted, first_own).astype(BF16)
        parts[units + unit] = dot_first(grad_b, second).astype(BF16)
        if unit > 0:
            back = jnp.dot(shifted, flat[unit], preferred_element_type=F32).astype(BF16)
            grad_first = lax.psum_scatter(back, "chan", scatter_dimension=1, tiled=True).astype(F32)
            grad_out = grad_out + grad_first * snake_slope(hidden_in, snake_freq_dilated[unit])
    sums = lax.psum(parts, "tm")
    dil = flat.astype(F32) * jnp.stack(sums[:units]).astype(F32)
    return outputs(hidden, dil, jnp.stack(sums[units:]))


def solution(mesh):
    return jax.shard_map(
        per_device,
        mesh=mesh,
        in_specs=(
            P("chan", "tm"),
            P(None, "chan", "tm"),
            P(None, None, "chan", None),
            P(None, "chan", None),
            P(None, None, "chan", None),
            P(None, "chan", None),
            P("chan"),
            P(None, "chan"),
            P(None, "chan"),
            P(),
            P("chan", "tm"),
        ),
        out_specs=(P("chan", "tm"), P(None, None, "chan", None), P(None, "chan", None)),
        check_vma=False,
    )
```
